128 devices in a mesh: dp: 16 (over z, y_hi, core), tensor: 8 (over x, y_lo).
Axes of the slice: x: 4, y: 4 (y_hi: 2, y_lo: 2; y = y_hi * 2 + y_lo), z: 4, core: 2. Of those that a mesh axis runs over, the one named last changes fastest.
Arguments:
- prefix_in: bfloat16 [8192, 4608], P(('dp', 'tensor')), may hold values from -24 to 24
- action_in: bfloat16 [768, 2048], P('dp'), may hold values from -6 to 6
- segment_ids: int32 [16, 512], P('dp'), may hold values from 0 to 7, never falling along the last dimension, each value on 1 to 128 neighbouring positions
- gain_prefix: float32 [4608], replicated, may hold values from 0.5 to 1.5
- gain_action: float32 [2048], replicated, may hold values from 0.5 to 1.5
- query_prefix: bfloat16 [4608, 4096], P(None, 'tensor'), may hold values from -0.7365696 to 0.7365696
- key_prefix: bfloat16 [4608, 2048], P(None, 'tensor'), may hold values from -0.19150809 to 0.19150809
- value_prefix: bfloat16 [4608, 2048], P(None, 'tensor'), may hold values from -0.09375 to 0.09375
- out_prefix: bfloat16 [4608, 4096], P(None, 'tensor'), may hold values from -0.09375 to 0.09375
- query_action: bfloat16 [2048, 4096], P(None, 'tensor'), may hold values from -1.1048543 to 1.1048543
- key_action: bfloat16 [2048, 2048], P(None, 'tensor'), may hold values from -0.28726213 to 0.28726213
- value_action: bfloat16 [2048, 2048], P(None, 'tensor'), may hold values from -0.125 to 0.125
- out_action: bfloat16 [2048, 4096], P(None, 'tensor'), may hold values from -0.125 to 0.125
- cot_prefix: bfloat16 [8192, 4608], P(('dp', 'tensor')), may hold values from -6 to 6
- cot_action: bfloat16 [768, 2048], P('dp'), may hold values from -6 to 6
Outputs:
- prefix_grad: bfloat16 [8192, 4608], P(('dp', 'tensor'))
- action_grad: bfloat16 [768, 2048], P('dp')
- query_prefix_grad: bfloat16 [4608, 4096], P('dp', 'tensor')
- key_prefix_grad: bfloat16 [4608, 2048], P('dp', 'tensor')
- value_prefix_grad: bfloat16 [4608, 2048], P('dp', 'tensor')
- out_prefix_grad: bfloat16 [4608, 4096], P('dp', 'tensor')
- query_action_grad: bfloat16 [2048, 4096], P('dp', 'tensor')
- key_action_grad: bfloat16 [2048, 2048], P('dp', 'tensor')
- value_action_grad: bfloat16 [2048, 2048], P('dp', 'tensor')
- out_action_grad: bfloat16 [2048, 4096], P('dp', 'tensor')
The draws below stay inside these ranges and needn't reach their ends.
Inputs may be any that keep to these rules, and one draw needn't show every extreme that they name: `segment_ids`: along each sample's positions the ids never fall.
All inputs are finite; a program needn't handle non-finite values.
Results may differ from the reference program's by a relative error of at most 0.02.
The reference program's roundings to bfloat16 on the way count: a program that leaves them out, or rounds other values in their place, can miss the bound.
Values may be sent and summed in bfloat16 or wider, within the bound.
A program may use at most 192 MiB of HBM per device.

```python
import math
import jax
import jax.numpy as jnp
import numpy as np
from jax import lax

D = 4608
H = 32
KV = 16
HD = 128
DA = 2048
PREF = 512
ACT = 48
PREF_ALL = 8192
ACT_ALL = 768
N_DP = 16


def head_factors(key, heads, top):
    ranks = jax.random.permutation(key, heads).astype(jnp.float32)
    ladder = jnp.exp(ranks * (math.log(top) / max(heads - 1, 1)))
    return jnp.repeat(ladder, HD)


def scaled_weight(entries, factors, fan_in):
    return (entries * factors[None, :] * fan_in ** (-0.5)).astype(jnp.bfloat16)


def draw_query_prefix(key, part):
    key = jax.random.fold_in(key, 11)
    entry_key, head_key = jax.random.split(key)
    entries = jnp.clip(jax.random.normal(entry_key, (D, H * HD), jnp.float32), -6.0, 6.0)
    return scaled_weight(entries, head_factors(head_key, H, 8.0), D)


def draw_key_prefix(key, part):
    key = jax.random.fold_in(key, 12)
    entry_key, head_key = jax.random.split(key)
    entries = jnp.clip(jax.random.normal(entry_key, (D, KV * HD), jnp.float32), -6.0, 6.0)
    return scaled_weight(entries, head_factors(head_key, KV, 2.0), D)


def draw_query_action(key, part):
    key = jax.random.fold_in(key, 13)
    entry_key, head_key = jax.random.split(key)
    entries = jnp.clip(jax.random.normal(entry_key, (DA, H * HD), jnp.float32), -6.0, 6.0)
    return scaled_weight(entries, head_factors(head_key, H, 8.0), DA)


def draw_key_action(key, part):
    key = jax.random.fold_in(key, 14)
    entry_key, head_key = jax.random.split(key)
    entries = jnp.clip(jax.random.normal(entry_key, (DA, KV * HD), jnp.float32), -6.0, 6.0)
    return scaled_weight(entries, head_factors(head_key, KV, 2.0), DA)


def strengthened(values, own_key, source, target, shards_of, factor):
    def block_of(position):
        return (jnp.arange(values.shape[position]) // (values.shape[position] // shards_of)).reshape((-1,) + (1,) * (values.ndim - 1 - position))

    near = jax.random.permutation(own_key, shards_of)[block_of(target)]
    far = (block_of(target) + shards_of // 2) % shards_of
    return jnp.where((block_of(source) == near) | (block_of(source) == far), factor * values, values)


def shard_levels(own_key, dims, cuts, least, largest):
    loudness = 1.0
    for axis_at, blocks in cuts:
        draws = jax.random.uniform(jax.random.fold_in(jax.random.fold_in(own_key, 6), axis_at), (blocks,), jnp.float32, least / len(cuts), largest / len(cuts))
        loudness = loudness * jnp.repeat(jnp.exp(draws), dims[axis_at] // blocks).reshape((-1,) + (1,) * (len(dims) - 1 - axis_at))
    return loudness


def profile(amount, total, reach, lean):
    portions = [(1 << 20) // math.isqrt(standing ** lean) + 1 for standing in range(2, amount + 1)]
    rest, given = total - reach - (amount - 1), [1] * (amount - 1)
    while rest > 0:
        candidates = [i for i in range(amount - 1) if given[i] < reach]
        whole, left = sum([portions[i] for i in candidates]), rest
        for i in candidates:
            extra = min(reach - given[i], max(1, left * portions[i] // whole), rest)
            given[i] = given[i] + extra
            rest = rest - extra
    return np.array([reach] + given)


def ragged(rng, count, total, reach, skew):
    if count == 2:
        one = jax.random.randint(rng, (), max(1, total - reach), min(reach, total - 1) + 1)
        return jnp.stack([one, total - one])
    sizes = jnp.asarray(profile(count, total, reach, skew), jnp.int32)
    pairs = (count - 1) // 2
    donor, receiver = sizes[1:1 + 2 * pairs:2], sizes[2:2 + 2 * pairs:2]
    margin = jnp.minimum(donor - 1, reach - receiver)
    shifted = jax.random.randint(jax.random.fold_in(rng, 1), (pairs,), 0, 1 << 20) % (margin + 1)
    sizes = sizes.at[1:1 + 2 * pairs:2].set(donor - shifted).at[2:2 + 2 * pairs:2].set(receiver + shifted)
    return sizes[jax.random.permutation(jax.random.fold_in(rng, 2), count)]


def gaussian(rng, dims, deviation, reach, shards=(), kind=jnp.bfloat16):
    level = shard_levels(rng, dims, shards, -0.22, 0.18) if shards else 1.0
    array = jax.random.normal(rng, dims, jnp.float32) * deviation * level
    return jnp.minimum(jnp.maximum(array, -reach), reach).astype(kind)


def gaussian_with(rng, extent, spread, limit, cuts, heavy, held_as=jnp.bfloat16):
    values = spread * jax.random.normal(rng, extent, jnp.float32)
    if cuts:
        values = values * shard_levels(rng, extent, cuts, -0.22, 0.18)
    return jnp.clip(strengthened(values, jax.random.fold_in(rng, 3), *heavy), -limit, limit).astype(held_as)


def setup_inputs(seed: int = 0) -> dict:
    splits = jax.random.split(jax.random.key(seed), 16)
    return {
        "prefix_in": gaussian_with(splits[0], (PREF_ALL, D), 1.0, 24.0, ((0, 128),), (0, 1, 128, 5.5)),
        "action_in": gaussian(splits[1], (ACT_ALL, DA), 1.0, 6.0, ((0, 16),)),
        "segment_ids": jax.vmap(lambda own: jnp.searchsorted(jnp.cumsum(ragged(own, 8, PREF, PREF // 4, 1)), jnp.arange(PREF), side="right"))(jax.random.split(splits[2], N_DP)).reshape((N_DP, PREF)).astype(jnp.int32),
        "gain_prefix": jnp.clip(1.0 + 0.1 * jax.random.normal(splits[3], (D,), jnp.float32), 0.5, 1.5),
        "gain_action": jnp.clip(1.0 + 0.1 * jax.random.normal(splits[4], (DA,), jnp.float32), 0.5, 1.5),
        "query_prefix": draw_query_prefix(jax.random.fold_in(splits[15], 71), 0),
        "key_prefix": draw_key_prefix(jax.random.fold_in(splits[15], 71), 0),
        "value_prefix": gaussian(splits[7], (D, KV * HD), D ** -0.5, 0.09375, ((1, 8),)),
        "out_prefix": gaussian(splits[8], (D, H * HD), D ** -0.5, 0.09375, ((1, 8),)),
        "query_action": draw_query_action(jax.random.fold_in(splits[15], 71), 0),
        "key_action": draw_key_action(jax.random.fold_in(splits[15], 71), 0),
        "value_action": gaussian(splits[11], (DA, KV * HD), DA ** -0.5, 0.125, ((1, 8),)),
        "out_action": gaussian(splits[12], (DA, H * HD), DA ** -0.5, 0.125, ((1, 8),)),
        "cot_prefix": gaussian(splits[13], (PREF_ALL, D), 1.0, 6.0, ((0, 128),)),
        "cot_action": gaussian(splits[14], (ACT_ALL, DA), 1.0, 6.0, ((0, 16),)),
    }


EPSILON = 1e-06
SOFT_CAP = 50.0

def norm_rows(inputs, gain):
    widened = inputs.astype(jnp.float32)
    inverse = lax.rsqrt(lax.optimization_barrier(jnp.mean(widened * widened, -1, keepdims=True)) + EPSILON)
    return (widened, inverse, (widened * inverse * gain).astype(jnp.bfloat16))

def norm_back(widened, inverse, gain, upstream):
    normed = widened * inverse
    scaled = upstream * gain
    return (inverse * (scaled - normed * lax.optimization_barrier(jnp.mean(scaled * normed, -1, keepdims=True)))).astype(jnp.bfloat16)

def project(inputs, weight):
    return jnp.dot(inputs, weight, preferred_element_type=jnp.float32).astype(jnp.bfloat16)

def by_heads(matrix):
    return matrix.reshape(matrix.shape[0], matrix.shape[1] // HD, HD)

def attend(queries, all_keys, all_values, grad_out, allowed):
    q_count, q_heads, head_width = queries.shape
    kv_heads = all_keys.shape[1]
    group_size = q_heads // kv_heads
    score_scale = 1.0 / math.sqrt(D // H)
    q_group = queries.astype(jnp.float32).reshape(q_count, kv_heads, group_size, head_width)
    key_wide = all_keys.astype(jnp.float32)
    value_wide = all_values.astype(jnp.float32)
    raw_scores = jnp.einsum('qkgd,jkd->kgqj', q_group, key_wide) * score_scale
    capped = SOFT_CAP * jnp.tanh(raw_scores / SOFT_CAP)
    weights = jnp.exp(capped)
    if allowed is not None:
        weights = jnp.where(allowed, weights, 0.0)
    probs = weights / lax.optimization_barrier(jnp.sum(weights, -1, keepdims=True))
    prob_half = probs.astype(jnp.bfloat16)
    attended = jnp.einsum('kgqj,jkd->qkgd', prob_half.astype(jnp.float32), value_wide)
    attended = attended.astype(jnp.bfloat16).reshape(q_count, q_heads * head_width)
    out_group = grad_out.astype(jnp.float32).reshape(q_count, kv_heads, group_size, head_width)
    grad_probs = jnp.einsum('qkgd,jkd->kgqj', out_group, value_wide)
    inner = lax.optimization_barrier(jnp.sum(probs * grad_probs, -1, keepdims=True))
    slope = 1.0 - capped / SOFT_CAP * (capped / SOFT_CAP)
    grad_raw = (probs * (grad_probs - inner) * slope * score_scale).astype(jnp.bfloat16)
    grad_wide = grad_raw.astype(jnp.float32)
    grad_queries = jnp.einsum('kgqj,jkd->qkgd', grad_wide, key_wide)
    grad_queries = grad_queries.astype(jnp.bfloat16).reshape(q_count, q_heads * head_width)
    grad_keys = jnp.einsum('kgqj,qkgd->jkd', grad_wide, q_group)
    grad_values = jnp.einsum('kgqj,qkgd->jkd', prob_half.astype(jnp.float32), out_group)
    return (attended, grad_queries, grad_keys, grad_values)

def outer_sum(left_rows, right_rows):
    return jnp.dot(left_rows.T, right_rows, preferred_element_type=jnp.float32)

def back_project(grad_rows, weight):
    return jnp.dot(grad_rows, weight.T, preferred_element_type=jnp.float32)

def reference(prefix_in, action_in, segment_ids, gain_prefix, gain_action, query_prefix, key_prefix, value_prefix, out_prefix, query_action, key_action, value_action, out_action, cot_prefix, cot_action):
    weight_list = (query_prefix, key_prefix, value_prefix, out_prefix, query_action, key_action, value_action, out_action)

    def one_sample(carry, inputs):
        pre_one, act_one, seg_row, cot_pre, cot_act = inputs
        pre_wide, pre_inv, pre_normed = norm_rows(pre_one, gain_prefix)
        act_wide, act_inv, act_normed = norm_rows(act_one, gain_action)
        pre_query = project(pre_normed, query_prefix)
        pre_key = project(pre_normed, key_prefix)
        pre_value = project(pre_normed, value_prefix)
        pre_dout = project(cot_pre, out_prefix)
        act_query = project(act_normed, query_action)
        act_key = project(act_normed, key_action)
        act_value = project(act_normed, value_action)
        act_dout = project(cot_act, out_action)
        allowed = seg_row[None, :] <= seg_row[:, None]
        pre_attn, pre_dquery, pre_dkey, pre_dvalue = attend(by_heads(pre_query), by_heads(pre_key), by_heads(pre_value), by_heads(pre_dout), allowed)
        joint_keys = jnp.concatenate([by_heads(pre_key), by_heads(act_key)], 0)
        joint_values = jnp.concatenate([by_heads(pre_value), by_heads(act_value)], 0)
        act_attn, act_dquery, joint_dkey, joint_dvalue = attend(by_heads(act_query), joint_keys, joint_values, by_heads(act_dout), None)
        seq_len = pre_one.shape[0]
        pre_dkey = (pre_dkey + joint_dkey[:seq_len]).astype(jnp.bfloat16).reshape(seq_len, -1)
        pre_dvalue = (pre_dvalue + joint_dvalue[:seq_len]).astype(jnp.bfloat16).reshape(seq_len, -1)
        act_dkey = joint_dkey[seq_len:].astype(jnp.bfloat16).reshape(act_one.shape[0], -1)
        act_dvalue = joint_dvalue[seq_len:].astype(jnp.bfloat16).reshape(act_one.shape[0], -1)
        sample_grads = (outer_sum(pre_normed, pre_dquery), outer_sum(pre_normed, pre_dkey), outer_sum(pre_normed, pre_dvalue), outer_sum(cot_pre, pre_attn), outer_sum(act_normed, act_dquery), outer_sum(act_normed, act_dkey), outer_sum(act_normed, act_dvalue), outer_sum(cot_act, act_attn))
        new_carry = tuple((total + grad.astype(jnp.bfloat16).astype(jnp.float32) for total, grad in zip(carry, sample_grads)))
        pre_up = back_project(pre_dquery, query_prefix) + back_project(pre_dkey, key_prefix) + back_project(pre_dvalue, value_prefix)
        act_up = back_project(act_dquery, query_action) + back_project(act_dkey, key_action) + back_project(act_dvalue, value_action)
        return (new_carry, (norm_back(pre_wide, pre_inv, gain_prefix, pre_up), norm_back(act_wide, act_inv, gain_action, act_up)))
    initial = tuple((jnp.zeros(weight.shape, jnp.float32) for weight in weight_list))
    stacked = (prefix_in.reshape(N_DP, PREF, D), action_in.reshape(N_DP, ACT, DA), segment_ids, cot_prefix.reshape(N_DP, PREF, D), cot_action.reshape(N_DP, ACT, DA))
    totals, (pre_grads, act_grads) = lax.scan(one_sample, initial, stacked)
    return (pre_grads.reshape(N_DP * PREF, D), act_grads.reshape(N_DP * ACT, DA), totals[0].astype(jnp.bfloat16), totals[1].astype(jnp.bfloat16), totals[2].astype(jnp.bfloat16), totals[3].astype(jnp.bfloat16), totals[4].astype(jnp.bfloat16), totals[5].astype(jnp.bfloat16), totals[6].astype(jnp.bfloat16), totals[7].astype(jnp.bfloat16))
```

```python
import functools
import math

import jax
import jax.numpy as jnp
from jax import lax
from jax.experimental import pallas as pl
from jax.experimental.pallas import tpu as pltpu
from jax.sharding import PartitionSpec as P

D = 4608
DA = 2048
H = 32
HD = 128
ROWS = 64
ACT = 48
SLOTS = 8
PREF = SLOTS * ROWS
QW, KW = 512, 256
COLS = 2 * QW + 2 * KW
HALF = COLS // 2
TILE = 256
EPSILON = 1e-06
SOFT_CAP = 50.0
SCALE = 1.0 / math.sqrt(D // H)
MESH = pl.DeviceIdType.MESH
BF16, F32 = jnp.bfloat16, jnp.float32
VMEM = pl.BlockSpec(memory_space=pltpu.VMEM)
ANY = pl.BlockSpec(memory_space=pl.ANY)


def x_step(k):
    return lax.axis_index("dp"), lax.rem(lax.axis_index("tensor") + 2 * k + 8, 8)


def z_step(k):
    return lax.rem(lax.axis_index("dp") + 4 * k + 16, 16), lax.axis_index("tensor")


def y_low():
    t = lax.axis_index("tensor")
    return lax.axis_index("dp"), t + 1 - 2 * lax.rem(t, 2)


def y_high():
    d = lax.axis_index("dp")
    return d + 2 - 4 * lax.rem(lax.div(d, 2), 2), lax.axis_index("tensor")


def sibling():
    d = lax.axis_index("dp")
    return d + 1 - 2 * lax.rem(d, 2), lax.axis_index("tensor")


def slot_order():
    t = lax.axis_index("tensor")
    x, y = lax.div(t, 2), lax.rem(t, 2)

    def at(step, row):
        return 2 * lax.rem(x + step + 4, 4) + row

    return jnp.stack(
        [at(0, y), at(0, 1 - y), at(-1, y), at(1, y), at(2, y), at(-1, 1 - y), at(1, 1 - y), at(2, 1 - y)]
    )


def greet(partners):
    barrier = pltpu.get_barrier_semaphore()
    for device in partners:
        pl.semaphore_signal(barrier, inc=1, device_id=device, device_id_type=MESH)
    pl.semaphore_wait(barrier, len(partners))


def remote(src, dst, send, recv, device):
    return pltpu.make_async_remote_copy(
        src_ref=src, dst_ref=dst, send_sem=send, recv_sem=recv, device_id=device, device_id_type=MESH
    )


def norm(rows, gain):
    widened = rows.astype(F32)
    inverse = lax.rsqrt(jnp.mean(widened * widened, -1, keepdims=True) + EPSILON)
    return (widened * inverse * gain).astype(BF16)


def gather_kernel(
    pin, cot, gain, ain, acot, again, wq, wk, wv, wo, aq, ak, av, ao,
    proj, aproj, g_norm, g_cot, s_norm, s_cot, a_norm, sa_norm, sa_cot,
    norm_v, cot_v, w_v, aw_v, send, recv, sib_send, sib_recv, local, w_sem, act_send, act_recv,
):
    weights = []
    for i, (ref, first) in enumerate(((aq, 0), (ak, QW), (av, QW + KW), (ao, QW + 2 * KW))):
        weights.append(pltpu.make_async_copy(ref, aw_v.at[:, pl.ds(first, ref.shape[1])], w_sem.at[i]))
    for i, (ref, first) in enumerate(((wq, 0), (wk, QW), (wv, QW + KW), (wo, QW + 2 * KW))):
        weights.append(pltpu.make_async_copy(ref, w_v.at[:, pl.ds(first, ref.shape[1])], w_sem.at[4 + i]))
    for copy in weights:
        copy.start()
    left, right, across, twin = x_step(-1), x_step(1), y_low(), sibling()
    greet((left, right, across, twin))

    arrays = ((norm_v, g_norm, s_norm), (cot_v, g_cot, s_cot))

    def hop(a, src, dst, device):
        held = arrays[a][0]
        return remote(held.at[src], held.at[dst], send.at[a, dst], recv.at[a, dst], device)

    hops = [
        {1: hop(a, 0, 1, across), 2: hop(a, 0, 2, right), 3: hop(a, 0, 3, left),
         4: hop(a, 2, 4, right) if a == 0 else hop(a, 3, 4, left),
         5: hop(a, 1, 5, right), 6: hop(a, 1, 6, left), 7: hop(a, 4, 7, across)}
        for a in range(2)
    ]
    twins = [
        [remote(held.at[s], far.at[s], sib_send.at[a, s], sib_recv.at[a, s], twin) for s in range(SLOTS)]
        for a, (held, _, far) in enumerate(arrays)
    ]
    stores = [
        [pltpu.make_async_copy(held.at[s], near.at[s], local.at[a, s]) for s in range(SLOTS)]
        for a, (held, near, _) in enumerate(arrays)
    ]

    def spread(a, s):
        twins[a][s].start()
        stores[a][s].start()

    cot_v[0] = cot[...]
    for s in (1, 2, 3):
        hops[1][s].start()
    norm_v[0] = norm(pin[...], gain[...])
    for s in (1, 2, 3):
        hops[0][s].start()
    spread(1, 0)
    spread(0, 0)

    a_norm[...] = norm(ain[...], again[...])
    act_twins = [
        remote(a_norm, sa_norm, act_send.at[0], act_recv.at[0], twin),
        remote(acot, sa_cot, act_send.at[1], act_recv.at[1], twin),
    ]
    for copy in act_twins:
        copy.start()
    for copy in weights[:4]:
        copy.wait()

    def act_project(rows, first):
        def step(j, carry):
            cols = pl.ds(pl.multiple_of(j * TILE, TILE), TILE)
            aproj[:, cols] = jnp.dot(rows[...], aw_v[:, cols], preferred_element_type=F32).astype(BF16)
            return carry

        lax.fori_loop(first, first + (4 if first == 0 else 2), step, 0)

    act_project(a_norm, 0)
    act_project(acot, 4)

    def project(held, low, high, first):
        def step(j, carry):
            cols = pl.ds(pl.multiple_of(j * TILE, TILE), TILE)
            rows = held[low:high].reshape((high - low) * ROWS, D)
            out = jnp.dot(rows, w_v[:, cols], preferred_element_type=F32).astype(BF16)
            proj[low:high, :, cols] = out.reshape(high - low, ROWS, TILE)
            return carry

        lax.fori_loop(first, first + (4 if first == 0 else 2), step, 0)

    hops[1][3].wait_recv()
    hops[1][4].start()
    hops[0][2].wait_recv()
    hops[0][4].start()
    for a in (1, 0):
        hops[a][1].wait_recv()
        hops[a][5].start()
        hops[a][6].start()
    hops[1][2].wait_recv()
    hops[0][3].wait_recv()
    for a in (1, 0):
        for s in (1, 2, 3):
            spread(a, s)
    for copy in weights[4:]:
        copy.wait()
    project(cot_v, 0, 4, 4)
    for a in (1, 0):
        hops[a][4].wait_recv()
        hops[a][7].start()
        spread(a, 4)
    project(norm_v, 0, 4, 0)
    for a, first in ((1, 4), (0, 0)):
        for s in (5, 6, 7):
            hops[a][s].wait_recv()
            spread(a, s)
        project(arrays[a][0], 4, 8, first)
    for a in range(2):
        for s in range(1, SLOTS):
            hops[a][s].wait_send()
        for s in range(SLOTS):
            twins[a][s].wait()
            stores[a][s].wait()
    for copy in act_twins:
        copy.wait()


def gather_and_project(pin, cot, gain, ain, acot, again, *weights):
    rows = jax.ShapeDtypeStruct((SLOTS, ROWS, D), BF16)
    acts = jax.ShapeDtypeStruct((ACT, DA), BF16)
    dma = pltpu.SemaphoreType.DMA
    return pl.pallas_call(
        gather_kernel,
        out_shape=(
            jax.ShapeDtypeStruct((SLOTS, ROWS, COLS), BF16), jax.ShapeDtypeStruct((ACT, COLS), BF16),
            rows, rows, rows, rows, acts, acts, acts,
        ),
        in_specs=[VMEM] * 6 + [ANY] * 8,
        out_specs=(VMEM, VMEM, ANY, ANY, ANY, ANY, VMEM, ANY, ANY),
        scratch_shapes=[
            pltpu.VMEM((SLOTS, ROWS, D), BF16), pltpu.VMEM((SLOTS, ROWS, D), BF16),
            pltpu.VMEM((D, COLS), BF16), pltpu.VMEM((DA, COLS), BF16),
            dma((2, SLOTS)), dma((2, SLOTS)), dma((2, SLOTS)), dma((2, SLOTS)), dma((2, SLOTS)),
            dma((8,)), dma((2,)), dma((2,)),
        ],
        compiler_params=pltpu.CompilerParams(
            collective_id=0, has_side_effects=True, vmem_limit_bytes=56 << 20
        ),
        name="gather_and_project",
    )(pin, cot, gain[None, :], ain, acot, again[None, :], *weights)


def dot_last(a, b):
    return lax.dot_general(a, b, (((1,), (1,)), ((), ())), preferred_element_type=F32)


def soft(key_rows, query_rows):
    t = jnp.tanh(dot_last(key_rows, query_rows) * (SCALE / SOFT_CAP))
    return t, jnp.exp(SOFT_CAP * t)


def attend_kernel(proj, aproj, seg_row, seg_col, grads, agrads, dk, dv):
    block = 256
    for h in range(2):
        key = proj[:, QW + HD * h : QW + HD * (h + 1)]
        value = proj[:, QW + KW + HD * h : QW + KW + HD * (h + 1)]
        key_t, value_t = key.T, value.T
        base = HALF * h
        akey = aproj[:, QW + HD * h : QW + HD * (h + 1)]
        avalue = aproj[:, QW + KW + HD * h : QW + KW + HD * (h + 1)]

        def two(first):
            return jnp.concatenate([aproj[:, first + HD * (2 * h + g) : first + HD * (2 * h + g + 1)] for g in range(2)], 0)

        aq, ado = two(0), two(QW + 2 * KW)
        tp, wp = soft(key, aq)
        ta, wa = soft(akey, aq)
        rate = 1.0 / (jnp.sum(wp, 0, keepdims=True) + jnp.sum(wa, 0, keepdims=True))
        pp, pa = wp * rate, wa * rate
        gp, ga = dot_last(value, ado), dot_last(avalue, ado)
        inner = jnp.sum(pp * gp, 0, keepdims=True) + jnp.sum(pa * ga, 0, keepdims=True)
        sp = (pp * (gp - inner) * (1.0 - tp * tp) * SCALE).astype(BF16)
        sa = (pa * (ga - inner) * (1.0 - ta * ta) * SCALE).astype(BF16)
        pp, pa = pp.astype(BF16), pa.astype(BF16)
        dk[...] = jnp.dot(sp, aq, preferred_element_type=F32)
        dv[...] = jnp.dot(pp, ado, preferred_element_type=F32)
        agrads[:, base + 256 : base + 384] = jnp.dot(sa, aq, preferred_element_type=F32).astype(BF16)
        agrads[:, base + 384 : base + 512] = jnp.dot(pa, ado, preferred_element_type=F32).astype(BF16)
        adq = (jnp.dot(key_t, sp, preferred_element_type=F32) + jnp.dot(akey.T, sa, preferred_element_type=F32)).T
        aat = (jnp.dot(value_t, pp, preferred_element_type=F32) + jnp.dot(avalue.T, pa, preferred_element_type=F32)).T
        for g in range(2):
            agrads[:, base + HD * g : base + HD * (g + 1)] = adq[ACT * g : ACT * (g + 1)].astype(BF16)
            agrads[:, base + 512 + HD * g : base + 512 + HD * (g + 1)] = aat[ACT * g : ACT * (g + 1)].astype(BF16)

        for g in range(2):
            for b in range(PREF // block):
                rows = slice(b * block, (b + 1) * block)
                first = HD * (2 * h + g)
                query = proj[rows, first : first + HD]
                dout = proj[rows, QW + 2 * KW + first : QW + 2 * KW + first + HD]
                t, w = soft(key, query)
                w = jnp.where(seg_col[...] <= seg_row[:, rows], w, 0.0)
                p = w * (1.0 / jnp.sum(w, 0, keepdims=True))
                gp = dot_last(value, dout)
                inner = jnp.sum(p * gp, 0, keepdims=True)
                s = (p * (gp - inner) * (1.0 - t * t) * SCALE).astype(BF16)
                p = p.astype(BF16)
                dk[...] += jnp.dot(s, query, preferred_element_type=F32)
                dv[...] += jnp.dot(p, dout, preferred_element_type=F32)
                dq = jnp.dot(key_t, s, preferred_element_type=F32).T
                at = jnp.dot(value_t, p, preferred_element_type=F32).T
                grads[rows, base + HD * g : base + HD * (g + 1)] = dq.astype(BF16)
                grads[rows, base + 512 + HD * g : base + 512 + HD * (g + 1)] = at.astype(BF16)
        grads[:, base + 256 : base + 384] = dk[...].astype(BF16)
        grads[:, base + 384 : base + 512] = dv[...].astype(BF16)


def attend(proj, aproj, seg):
    return pl.pallas_call(
        attend_kernel,
        out_shape=(jax.ShapeDtypeStruct((PREF, COLS), BF16), jax.ShapeDtypeStruct((ACT, COLS), BF16)),
        in_specs=[VMEM] * 4,
        out_specs=(VMEM, VMEM),
        scratch_shapes=[pltpu.VMEM((PREF, HD), F32), pltpu.VMEM((PREF, HD), F32)],
        compiler_params=pltpu.CompilerParams(vmem_limit_bytes=48 << 20),
        name="attend",
    )(proj, aproj, seg[None, :], seg[:, None])


def outer_sum(left_rows, right_rows):
    return lax.dot_general(left_rows, right_rows, (((0,), (0,)), ((), ())), preferred_element_type=F32)


def norm_back(rows, gain, upstream):
    widened = rows.astype(F32)
    inverse = lax.rsqrt(jnp.mean(widened * widened, -1, keepdims=True) + EPSILON)
    normed = widened * inverse
    scaled = upstream * gain
    return (inverse * (scaled - normed * jnp.mean(scaled * normed, -1, keepdims=True))).astype(BF16)


def columns(grads, what):
    first, width = {"q": (0, 256), "k": (256, 128), "v": (384, 128), "o": (512, 256)}[what]
    return jnp.concatenate([grads[:, HALF * h + first : HALF * h + first + width] for h in range(2)], 1)


def per_device(prefix_in, action_in, segment_ids, gain_prefix, gain_action, query_prefix, key_prefix, value_prefix,
               out_prefix, query_action, key_action, value_action, out_action, cot_prefix, cot_action):
    proj, aproj, g_norm, g_cot, s_norm, s_cot, a_norm, sa_norm, sa_cot = gather_and_project(
        prefix_in, cot_prefix, gain_prefix, action_in, cot_action, gain_action, query_prefix, key_prefix,
        value_prefix, out_prefix, query_action, key_action, value_action, out_action)
    order = slot_order()
    seg = segment_ids.reshape(SLOTS, ROWS)[order].reshape(PREF)
    grads, agrads = attend(proj.reshape(PREF, COLS), aproj, seg)
    rows, cots = g_norm.reshape(PREF, D), g_cot.reshape(PREF, D)
    terms = [outer_sum(cots if w == "o" else rows, columns(grads, w)) for w in "qkvo"]
    terms += [outer_sum(cot_action if w == "o" else a_norm, columns(agrads, w)) for w in "qkvo"]
    out = [lax.psum_scatter(t.astype(BF16), "dp", scatter_dimension=0, tiled=True) for t in terms]
    up = sum(dot_last(columns(grads, w), m) for w, m in zip("qkv", (query_prefix, key_prefix, value_prefix)))
    aup = sum(dot_last(columns(agrads, w), m) for w, m in zip("qkv", (query_action, key_action, value_action)))
    up = up.astype(BF16).reshape(SLOTS, ROWS, D)[jnp.argsort(order)].reshape(PREF, D)
    own = lax.psum_scatter(up, "tensor", scatter_dimension=0, tiled=True).astype(F32)
    total = lax.psum(aup.astype(BF16), "tensor").astype(F32)
    return (norm_back(prefix_in, gain_prefix, own), norm_back(action_in, gain_action, total), *out)


def solution(mesh):
    rows, sample, cols = P(("dp", "tensor"), None), P("dp", None), P(None, "tensor")
    in_specs = (rows, sample, sample, P(), P()) + (cols,) * 8 + (rows, sample)
    out_specs = (rows, sample) + (P("dp", "tensor"),) * 8
    return jax.shard_map(per_device, mesh=mesh, in_specs=in_specs, out_specs=out_specs, check_vma=False)
```

```python
import functools
import math

import jax
import jax.numpy as jnp
from jax import lax
from jax.experimental import pallas as pl
from jax.experimental.pallas import tpu as pltpu
from jax.sharding import PartitionSpec as P

D = 4608
DA = 2048
H = 32
HD = 128
ROWS = 64
ACT = 48
SLOTS = 8
PREF = SLOTS * ROWS
QW, KW = 512, 256
COLS = 2 * QW + 2 * KW
HALF = COLS // 2
TILE = 256
EPSILON = 1e-06
SOFT_CAP = 50.0
SCALE = 1.0 / math.sqrt(D // H)
MESH = pl.DeviceIdType.MESH
BF16, F32 = jnp.bfloat16, jnp.float32
VMEM = pl.BlockSpec(memory_space=pltpu.VMEM)
ANY = pl.BlockSpec(memory_space=pl.ANY)


def x_step(k):
    return lax.axis_index("dp"), lax.rem(lax.axis_index("tensor") + 2 * k + 8, 8)


def z_step(k):
    return lax.rem(lax.axis_index("dp") + 4 * k + 16, 16), lax.axis_index("tensor")


def y_low():
    t = lax.axis_index("tensor")
    return lax.axis_index("dp"), t + 1 - 2 * lax.rem(t, 2)


def y_high():
    d = lax.axis_index("dp")
    return d + 2 - 4 * lax.rem(lax.div(d, 2), 2), lax.axis_index("tensor")


def sibling():
    d = lax.axis_index("dp")
    return d + 1 - 2 * lax.rem(d, 2), lax.axis_index("tensor")


def slot_order():
    t = lax.axis_index("tensor")
    x, y = lax.div(t, 2), lax.rem(t, 2)

    def at(step, row):
        return 2 * lax.rem(x + step + 4, 4) + row

    return jnp.stack(
        [at(0, y), at(0, 1 - y), at(-1, y), at(1, y), at(2, y), at(-1, 1 - y), at(1, 1 - y), at(2, 1 - y)]
    )


def greet(partners):
    barrier = pltpu.get_barrier_semaphore()
    for device in partners:
        pl.semaphore_signal(barrier, inc=1, device_id=device, device_id_type=MESH)
    pl.semaphore_wait(barrier, len(partners))


def remote(src, dst, send, recv, device):
    return pltpu.make_async_remote_copy(
        src_ref=src, dst_ref=dst, send_sem=send, recv_sem=recv, device_id=device, device_id_type=MESH
    )


def norm(rows, gain):
    widened = rows.astype(F32)
    inverse = lax.rsqrt(jnp.mean(widened * widened, -1, keepdims=True) + EPSILON)
    return (widened * inverse * gain).astype(BF16)


def gather_kernel(
    pin, cot, gain, ain, acot, again, wq, wk, wv, wo, aq, ak, av, ao,
    proj, aproj, g_norm, g_cot, s_norm, s_cot, a_norm, sa_norm, sa_cot,
    norm_v, cot_v, w_v, aw_v, send, recv, sib_send, sib_recv, local, w_sem, act_send, act_recv,
):
    weights = []
    for i, (ref, first) in enumerate(((aq, 0), (ak, QW), (av, QW + KW), (ao, QW + 2 * KW))):
        weights.append(pltpu.make_async_copy(ref, aw_v.at[:, pl.ds(first, ref.shape[1])], w_sem.at[i]))
    for i, (ref, first) in enumerate(((wq, 0), (wk, QW), (wv, QW + KW), (wo, QW + 2 * KW))):
        weights.append(pltpu.make_async_copy(ref, w_v.at[:, pl.ds(first, ref.shape[1])], w_sem.at[4 + i]))
    for copy in weights:
        copy.start()
    left, right, across, twin = x_step(-1), x_step(1), y_low(), sibling()
    greet((left, right, across, twin))

    arrays = ((norm_v, g_norm, s_norm), (cot_v, g_cot, s_cot))

    def hop(a, src, dst, device):
        held = arrays[a][0]
        return remote(held.at[src], held.at[dst], send.at[a, dst], recv.at[a, dst], device)

    hops = [
        {1: hop(a, 0, 1, across), 2: hop(a, 0, 2, right), 3: hop(a, 0, 3, left),
         4: hop(a, 2, 4, right) if a == 0 else hop(a, 3, 4, left),
         5: hop(a, 1, 5, right), 6: hop(a, 1, 6, left), 7: hop(a, 4, 7, across)}
        for a in range(2)
    ]
    twins = [
        [remote(held.at[s], far.at[s], sib_send.at[a, s], sib_recv.at[a, s], twin) for s in range(SLOTS)]
        for a, (held, _, far) in enumerate(arrays)
    ]
    stores = [
        [pltpu.make_async_copy(held.at[s], near.at[s], local.at[a, s]) for s in range(SLOTS)]
        for a, (held, near, _) in enumerate(arrays)
    ]

    def spread(a, s):
        twins[a][s].start()
        stores[a][s].start()

    cot_v[0] = cot[...]
    for s in (1, 2, 3):
        hops[1][s].start()
    norm_v[0] = norm(pin[...], gain[...])
    for s in (1, 2, 3):
        hops[0][s].start()
    spread(1, 0)
    spread(0, 0)

    a_norm[...] = norm(ain[...], again[...])
    act_twins = [
        remote(a_norm, sa_norm, act_send.at[0], act_recv.at[0], twin),
        remote(acot, sa_cot, act_send.at[1], act_recv.at[1], twin),
    ]
    for copy in act_twins:
        copy.start()
    for copy in weights[:4]:
        copy.wait()

    def act_project(rows, first):
        def step(j, carry):
            cols = pl.ds(pl.multiple_of(j * TILE, TILE), TILE)
            aproj[:, cols] = jnp.dot(rows[...], aw_v[:, cols], preferred_element_type=F32).astype(BF16)
            return carry

        lax.fori_loop(first, first + (4 if first == 0 else 2), step, 0)

    act_project(a_norm, 0)
    act_project(acot, 4)

    def project(held, low, high, first):
        def step(j, carry):
            cols = pl.ds(pl.multiple_of(j * TILE, TILE), TILE)
            rows = held[low:high].reshape((high - low) * ROWS, D)
            out = jnp.dot(rows, w_v[:, cols], preferred_element_type=F32).astype(BF16)
            proj[low:high, :, cols] = out.reshape(high - low, ROWS, TILE)
            return carry

        lax.fori_loop(first, first + (4 if first == 0 else 2), step, 0)

    hops[1][3].wait_recv()
    hops[1][4].start()
    hops[0][2].wait_recv()
    hops[0][4].start()
    for a in (1, 0):
        hops[a][1].wait_recv()
        hops[a][5].start()
        hops[a][6].start()
    hops[1][2].wait_recv()
    hops[0][3].wait_recv()
    for a in (1, 0):
        for s in (1, 2, 3):
            spread(a, s)
    for copy in weights[4:]:
        copy.wait()
    project(cot_v, 0, 4, 4)
    for a in (1, 0):
        hops[a][4].wait_recv()
        hops[a][7].start()
        spread(a, 4)
    project(norm_v, 0, 4, 0)
    for a, first in ((1, 4), (0, 0)):
        for s in (5, 6, 7):
            hops[a][s].wait_recv()
            spread(a, s)
        project(arrays[a][0], 4, 8, first)
    for a in range(2):
        for s in range(1, SLOTS):
            hops[a][s].wait_send()
        for s in range(SLOTS):
            twins[a][s].wait()
            stores[a][s].wait()
    for copy in act_twins:
        copy.wait()


def gather_and_project(pin, cot, gain, ain, acot, again, *weights):
    rows = jax.ShapeDtypeStruct((SLOTS, ROWS, D), BF16)
    acts = jax.ShapeDtypeStruct((ACT, DA), BF16)
    dma = pltpu.SemaphoreType.DMA
    return pl.pallas_call(
        gather_kernel,
        out_shape=(
            jax.ShapeDtypeStruct((SLOTS, ROWS, COLS), BF16), jax.ShapeDtypeStruct((ACT, COLS), BF16),
            rows, rows, rows, rows, acts, acts, acts,
        ),
        in_specs=[VMEM] * 6 + [ANY] * 8,
        out_specs=(VMEM, VMEM, ANY, ANY, ANY, ANY, VMEM, ANY, ANY),
        scratch_shapes=[
            pltpu.VMEM((SLOTS, ROWS, D), BF16), pltpu.VMEM((SLOTS, ROWS, D), BF16),
            pltpu.VMEM((D, COLS), BF16), pltpu.VMEM((DA, COLS), BF16),
            dma((2, SLOTS)), dma((2, SLOTS)), dma((2, SLOTS)), dma((2, SLOTS)), dma((2, SLOTS)),
            dma((8,)), dma((2,)), dma((2,)),
        ],
        compiler_params=pltpu.CompilerParams(
            collective_id=0, has_side_effects=True, vmem_limit_bytes=56 << 20
        ),
        name="gather_and_project",
    )(pin, cot, gain[None, :], ain, acot, again[None, :], *weights)


def dot_last(a, b):
    return lax.dot_general(a, b, (((1,), (1,)), ((), ())), preferred_element_type=F32)


def soft(key_rows, query_rows):
    t = jnp.tanh(dot_last(key_rows, query_rows) * (SCALE / SOFT_CAP))
    return t, jnp.exp(SOFT_CAP * t)


def attend_kernel(proj, aproj, seg_row, seg_col, grads, agrads, dk, dv):
    block = 256
    for h in range(2):
        key = proj[:, QW + HD * h : QW + HD * (h + 1)]
        value = proj[:, QW + KW + HD * h : QW + KW + HD * (h + 1)]
        key_t, value_t = key.T, value.T
        base = HALF * h
        akey = aproj[:, QW + HD * h : QW + HD * (h + 1)]
        avalue = aproj[:, QW + KW + HD * h : QW + KW + HD * (h + 1)]

        def two(first):
            return jnp.concatenate([aproj[:, first + HD * (2 * h + g) : first + HD * (2 * h + g + 1)] for g in range(2)], 0)

        aq, ado = two(0), two(QW + 2 * KW)
        tp, wp = soft(key, aq)
        ta, wa = soft(akey, aq)
        rate = 1.0 / (jnp.sum(wp, 0, keepdims=True) + jnp.sum(wa, 0, keepdims=True))
        pp, pa = wp * rate, wa * rate
        gp, ga = dot_last(value, ado), dot_last(avalue, ado)
        inner = jnp.sum(pp * gp, 0, keepdims=True) + jnp.sum(pa * ga, 0, keepdims=True)
        sp = (pp * (gp - inner) * (1.0 - tp * tp) * SCALE).astype(BF16)
        sa = (pa * (ga - inner) * (1.0 - ta * ta) * SCALE).astype(BF16)
        pp, pa = pp.astype(BF16), pa.astype(BF16)
        dk[...] = jnp.dot(sp, aq, preferred_element_type=F32)
        dv[...] = jnp.dot(pp, ado, preferred_element_type=F32)
        agrads[:, base + 256 : base + 384] = jnp.dot(sa, aq, preferred_element_type=F32).astype(BF16)
        agrads[:, base + 384 : base + 512] = jnp.dot(pa, ado, preferred_element_type=F32).astype(BF16)
        adq = (jnp.dot(key_t, sp, preferred_element_type=F32) + jnp.dot(akey.T, sa, preferred_element_type=F32)).T
        aat = (jnp.dot(value_t, pp, preferred_element_type=F32) + jnp.dot(avalue.T, pa, preferred_element_type=F32)).T
        for g in range(2):
            agrads[:, base + HD * g : base + HD * (g + 1)] = adq[ACT * g : ACT * (g + 1)].astype(BF16)
            agrads[:, base + 512 + HD * g : base + 512 + HD * (g + 1)] = aat[ACT * g : ACT * (g + 1)].astype(BF16)

        for g in range(2):
            for b in range(PREF // block):
                rows = slice(b * block, (b + 1) * block)
                first = HD * (2 * h + g)
                query = proj[rows, first : first + HD]
                dout = proj[rows, QW + 2 * KW + first : QW + 2 * KW + first + HD]
                t, w = soft(key, query)
                w = jnp.where(seg_col[...] <= seg_row[:, rows], w, 0.0)
                p = w * (1.0 / jnp.sum(w, 0, keepdims=True))
                gp = dot_last(value, dout)
                inner = jnp.sum(p * gp, 0, keepdims=True)
                s = (p * (gp - inner) * (1.0 - t * t) * SCALE).astype(BF16)
                p = p.astype(BF16)
                dk[...] += jnp.dot(s, query, preferred_element_type=F32)
                dv[...] += jnp.dot(p, dout, preferred_element_type=F32)
                dq = jnp.dot(key_t, s, preferred_element_type=F32).T
                at = jnp.dot(value_t, p, preferred_element_type=F32).T
                grads[rows, base + HD * g : base + HD * (g + 1)] = dq.astype(BF16)
                grads[rows, base + 512 + HD * g : base + 512 + HD * (g + 1)] = at.astype(BF16)
        grads[:, base + 256 : base + 384] = dk[...].astype(BF16)
        grads[:, base + 384 : base + 512] = dv[...].astype(BF16)


def attend(proj, aproj, seg):
    return pl.pallas_call(
        attend_kernel,
        out_shape=(jax.ShapeDtypeStruct((PREF, COLS), BF16), jax.ShapeDtypeStruct((ACT, COLS), BF16)),
        in_specs=[VMEM] * 4,
        out_specs=(VMEM, VMEM),
        scratch_shapes=[pltpu.VMEM((PREF, HD), F32), pltpu.VMEM((PREF, HD), F32)],
        compiler_params=pltpu.CompilerParams(vmem_limit_bytes=48 << 20),
        name="attend",
    )(proj, aproj, seg[None, :], seg[:, None])


SHARE = 416
PRE, ACTS = 288, 128
Z_PRE, Z_ACT = 4 * PRE, 4 * ACTS
LHS_TILE = 384
UP_TILE = 512


def add(*terms):
    total = terms[0].astype(F32)
    for term in terms[1:]:
        total = total + term.astype(F32)
    return total


def norm_back(rows, gain, upstream):
    widened = rows.astype(F32)
    inverse = lax.rsqrt(jnp.mean(widened * widened, -1, keepdims=True) + EPSILON)
    normed = widened * inverse
    scaled = upstream * gain
    return (inverse * (scaled - normed * jnp.mean(scaled * normed, -1, keepdims=True))).astype(BF16)


def sum_kernel(
    g_norm, g_cot, s_norm, s_cot, a_norm, acot, sa_norm, sa_cot, grads, agrads, pin, gain, ain, again,
    wq, wk, wv, aq, ak, av,
    pgrad, agrad, final,
    left_v, act_v, right_v, aright_v, w_v, part, z1_v, z2_v, y_v, done_v, up_v, u1_v, u2_v, uy_v, aup_v, ay_v, ax_v,
    load_sem, w_sem, ex_send, ex_recv, z1_send, z1_recv, z2_send, z2_recv, y_send, y_recv, f_send, f_recv, f_local,
    u1_send, u1_recv, u2_send, u2_recv, uy_send, uy_recv, ay_send, ay_recv, ax_send, ax_recv,
):
    d = lax.axis_index("dp")
    z, yh, core = lax.div(d, 4), lax.rem(lax.div(d, 2), 2), lax.rem(d, 2)
    steps = (2, 1, -1, 0)
    z_of = [lax.rem(z + s + 4, 4) for s in steps]

    loads = {}
    for r in range(4):
        for a, pair in enumerate(((g_norm, s_norm), (g_cot, s_cot))):
            cols = pl.ds(pl.multiple_of(z_of[r] * Z_PRE, 128), Z_PRE)
            loads[a, r] = [
                pltpu.make_async_copy(
                    ref.at[:, cols], left_v.at[a, r, pl.ds(PREF * i, PREF)], load_sem.at[a, r, i])
                for i, ref in enumerate(pair)
            ]
    for key in ((0, 0), (0, 1), (0, 2), (1, 0), (0, 3), (1, 1), (1, 2), (1, 3)):
        for copy in loads[key]:
            copy.start()

    def w_copies(refs, t, slot):
        rows = pl.ds(pl.multiple_of(t * UP_TILE, UP_TILE), UP_TILE)
        copies = []
        for h in range(2):
            for j, (ref, width, first) in enumerate(zip(refs, (256, 128, 128), (0, 256, 384))):
                copies.append(pltpu.make_async_copy(
                    ref.at[rows, pl.ds(width * h, width)],
                    w_v.at[slot, :, pl.ds(UP_TILE * h + first, width)],
                    w_sem.at[slot, 3 * h + j]))
        return copies

    z_right, z_left, across, twin = z_step(1), z_step(-1), y_high(), sibling()
    x_right, x_left, x_far, y_near = x_step(1), x_step(-1), x_step(2), y_low()
    greet((z_right, z_left, across, twin, x_right, x_left, x_far, y_near))

    mine = pl.ds(pl.multiple_of(core * HALF, HALF), HALF)
    theirs = pl.ds(pl.multiple_of((1 - core) * HALF, HALF), HALF)
    exchange = [
        remote(grads.at[:, theirs], right_v.at[pl.ds(PREF, PREF)], ex_send.at[0], ex_recv.at[0], twin),
        remote(agrads.at[:, theirs], aright_v.at[pl.ds(ACT, ACT)], ex_send.at[1], ex_recv.at[1], twin),
    ]
    for copy in exchange:
        copy.start()
    right_v[0:PREF] = grads[:, mine]
    aright_v[0:ACT] = agrads[:, mine]
    act_v[0, 0:ACT] = a_norm[...]
    act_v[0, ACT : 2 * ACT] = sa_norm[...]
    act_v[1, 0:ACT] = acot[...]
    act_v[1, ACT : 2 * ACT] = sa_cot[...]

    loaded = set()

    def weight_grad(g, r):
        a = 0 if g < 2 else 1
        if (a, r) not in loaded:
            loaded.add((a, r))
            for copy in loads[a, r]:
                copy.wait()
        cols = slice(256 * g, 256 * (g + 1))
        for t in range(Z_PRE // LHS_TILE):
            low, high = t * LHS_TILE, (t + 1) * LHS_TILE
            out = lax.dot_general(
                left_v[a, r, :, low:high], right_v[:, cols], (((0,), (0,)), ((), ())), preferred_element_type=F32
            ).astype(BF16)
            for share in range(4):
                first, last = max(low, PRE * share), min(high, PRE * (share + 1))
                if first < last:
                    part[g, r, share // 2, share % 2, first - PRE * share : last - PRE * share] = (
                        out[first - low : last - low])
        out = lax.dot_general(
            act_v[a, :, pl.ds(pl.multiple_of(z_of[r] * Z_ACT, Z_ACT), Z_ACT)], aright_v[:, cols],
            (((0,), (0,)), ((), ())), preferred_element_type=F32,
        ).astype(BF16)
        for share in range(4):
            part[g, r, share // 2, share % 2, PRE:SHARE] = out[ACTS * share : ACTS * (share + 1)]

    z1 = [
        [remote(part.at[g, 0, i], z1_v.at[g, i], z1_send.at[g, i], z1_recv.at[g, i], (z_right, z_left)[i])
         for i in range(2)] for g in range(3)
    ]
    z2 = [
        [[remote(part.at[g, 1 + i, y], z2_v.at[g, i, y], z2_send.at[g, i, y], z2_recv.at[g, i, y],
                 (z_right, z_left)[i]) for y in range(2)] for i in range(2)] for g in range(3)
    ]
    ys = [remote(part.at[g, 3, 1 - yh], y_v.at[g], y_send.at[g], y_recv.at[g], across) for g in range(3)]
    outs = [
        remote(done_v.at[g, 1 - core], final.at[core, g], f_send.at[g], f_recv.at[g], twin) for g in range(3)
    ]
    kept = [pltpu.make_async_copy(done_v.at[g, core], final.at[core, g], f_local.at[g]) for g in range(3)]

    def z_first(g):
        weight_grad(g, 0)
        for copy in z1[g]:
            copy.start()

    def z_raw(g):
        weight_grad(g, 1)
        z2[g][0][1].start()
        weight_grad(g, 2)
        z2[g][1][0].start()

    def z_second(g):
        for i in range(2):
            z1[g][i].wait_recv()
            part[g, 1 + i, i] = add(part[g, 1 + i, i], z1_v[g, i]).astype(BF16)
            z2[g][i][i].start()

    def y_first(g):
        for i in range(2):
            for y in range(2):
                z2[g][i][y].wait_recv()
        y = 1 - yh
        part[g, 3, y] = add(part[g, 3, y], z2_v[g, 0, y], z2_v[g, 1, y]).astype(BF16)
        ys[g].start()

    def finish(g):
        ys[g].wait_recv()
        done_v[g] = add(part[g, 3, yh], z2_v[g, 0, yh], z2_v[g, 1, yh], y_v[g]).astype(BF16)
        outs[g].start()
        kept[g].start()

    def up_loop(refs, count, use):
        def step(t, carry):
            slot = lax.rem(t, 2)

            @pl.when(t + 1 < count)
            def _():
                for copy in w_copies(refs, t + 1, 1 - slot):
                    copy.start()

            for copy in w_copies(refs, t, slot):
                copy.wait()
            use(t, slot)
            return carry

        for copy in w_copies(refs, 0, 0):
            copy.start()
        lax.fori_loop(0, count, step, 0)

    def through(cots, slot):
        return dot_last(cots[:, 0:UP_TILE], w_v[slot, :, 0:UP_TILE]) + dot_last(
            cots[:, HALF : HALF + UP_TILE], w_v[slot, :, UP_TILE : 2 * UP_TILE])

    def use_pre(t, slot):
        cols = pl.ds(pl.multiple_of(t * UP_TILE, UP_TILE), UP_TILE)
        up_v[:, :, cols] = through(grads, slot).astype(BF16).reshape(SLOTS, ROWS, UP_TILE)

    def use_act(t, slot):
        cols = pl.ds(pl.multiple_of(t * UP_TILE, UP_TILE), UP_TILE)
        aup_v[:, cols] = through(agrads, slot).astype(BF16)

    u1 = [
        remote(up_v.at[4], u1_v.at[0], u1_send.at[0], u1_recv.at[0], x_right),
        remote(up_v.at[7], u1_v.at[1], u1_send.at[1], u1_recv.at[1], x_left),
    ]
    u2 = [
        remote(up_v.at[s], u2_v.at[i], u2_send.at[i], u2_recv.at[i], device)
        for i, (s, device) in enumerate(((3, x_right), (6, x_right), (2, x_left), (5, x_left)))
    ]
    uy = remote(up_v.at[1], uy_v, uy_send.at[0], uy_recv.at[0], y_near)
    ay = remote(aup_v, ay_v, ay_send.at[0], ay_recv.at[0], y_near)
    ax = [
        remote(ax_v.at[0], ax_v.at[1 + i], ax_send.at[i], ax_recv.at[i], device)
        for i, device in enumerate((x_right, x_left, x_far))
    ]

    for copy in exchange:
        copy.wait_recv()
    z_first(0)
    z_raw(0)
    z_first(1)
    up_loop((aq, ak, av), DA // UP_TILE, use_act)
    ay.start()
    up_loop((wq, wk, wv), D // UP_TILE, use_pre)
    for copy in u1:
        copy.start()
    u2[1].start()
    u2[2].start()
    z_second(0)
    z_raw(1)
    z_first(2)
    weight_grad(0, 3)
    ay.wait_recv()
    ax_v[0] = add(aup_v[...], ay_v[...]).astype(BF16)
    for copy in ax:
        copy.start()
    for i, s in ((0, 3), (1, 5)):
        u1[i].wait_recv()
        up_v[s] = add(up_v[s], u1_v[i]).astype(BF16)
    u2[0].start()
    u2[3].start()
    z_second(1)
    z_raw(2)
    weight_grad(1, 3)
    weight_grad(2, 3)
    y_first(0)
    z_second(2)
    for copy in ax:
        copy.wait_recv()
    agrad[...] = norm_back(ain[...], again[...], add(ax_v[0], ax_v[3]) + add(ax_v[1], ax_v[2]))
    for copy in u2:
        copy.wait_recv()
    up_v[1] = add(up_v[1], u2_v[1], u2_v[3]).astype(BF16)
    uy.start()
    finish(0)
    y_first(1)
    uy.wait_recv()
    pgrad[...] = norm_back(pin[...], gain[...], add(up_v[0], u2_v[0], u2_v[2], uy_v[...]))
    finish(1)
    y_first(2)
    finish(2)

    for copy in (*exchange, *u1, *u2, uy, ay, *ax):
        copy.wait_send()
    for g in range(3):
        for i in range(2):
            z1[g][i].wait_send()
            for y in range(2):
                z2[g][i][y].wait_send()
        ys[g].wait_send()
        outs[g].wait()
        kept[g].wait()


def sum_everything(g_norm, g_cot, s_norm, s_cot, *rest):
    wide = tuple(m.reshape(PREF, D) for m in (g_norm, g_cot, s_norm, s_cot))
    dma = pltpu.SemaphoreType.DMA
    share = (2, SHARE, 256)
    row = (ROWS, D)

    def held(*shape):
        return pltpu.VMEM(shape, BF16)

    return pl.pallas_call(
        sum_kernel,
        out_shape=(
            jax.ShapeDtypeStruct(row, BF16), jax.ShapeDtypeStruct((ACT, DA), BF16),
            jax.ShapeDtypeStruct((2, 3, SHARE, 256), BF16),
        ),
        in_specs=[ANY] * 4 + [VMEM] * 10 + [ANY] * 6,
        out_specs=(VMEM, VMEM, ANY),
        scratch_shapes=[
            held(2, 4, 2 * PREF, Z_PRE), held(2, 2 * ACT, DA), held(2 * PREF, HALF), held(2 * ACT, HALF),
            held(2, UP_TILE, 2 * UP_TILE), held(3, 4, 2, *share), held(3, 2, *share), held(3, 2, 2, *share),
            held(3, *share), held(3, *share), held(SLOTS, *row), held(2, *row), held(4, *row), held(*row),
            held(ACT, DA), held(ACT, DA), held(4, ACT, DA),
            dma((2, 4, 2)), dma((2, 6)), dma((2,)), dma((2,)), dma((3, 2)), dma((3, 2)), dma((3, 2, 2)), dma((3, 2, 2)),
            dma((3,)), dma((3,)), dma((3,)), dma((3,)), dma((3,)),
            dma((2,)), dma((2,)), dma((4,)), dma((4,)), dma((1,)), dma((1,)), dma((1,)), dma((1,)), dma((3,)), dma((3,)),
        ],
        compiler_params=pltpu.CompilerParams(
            collective_id=1, has_side_effects=True, vmem_limit_bytes=62 << 20
        ),
        name="sum_everything",
    )(*wide, *rest)


def per_device(prefix_in, action_in, segment_ids, gain_prefix, gain_action, query_prefix, key_prefix, value_prefix,
               out_prefix, query_action, key_action, value_action, out_action, cot_prefix, cot_action):
    proj, aproj, g_norm, g_cot, s_norm, s_cot, a_norm, sa_norm, sa_cot = gather_and_project(
        prefix_in, cot_prefix, gain_prefix, action_in, cot_action, gain_action, query_prefix, key_prefix,
        value_prefix, out_prefix, query_action, key_action, value_action, out_action)
    seg = segment_ids.reshape(SLOTS, ROWS)[slot_order()].reshape(PREF)
    grads, agrads = attend(proj.reshape(PREF, COLS), aproj, seg)
    prefix_grad, action_grad, final = sum_everything(
        g_norm, g_cot, s_norm, s_cot, a_norm, cot_action, sa_norm, sa_cot, grads, agrads,
        prefix_in, gain_prefix[None, :], action_in, gain_action[None, :],
        query_prefix, key_prefix, value_prefix, query_action, key_action, value_action)

    def both(g, rows, cols):
        return jnp.concatenate([final[0, g, rows, cols], final[1, g, rows, cols]], 1)

    out = []
    for rows in (slice(0, PRE), slice(PRE, SHARE)):
        for g, cols in ((0, slice(0, 256)), (1, slice(0, 128)), (1, slice(128, 256)), (2, slice(0, 256))):
            out.append(both(g, rows, cols))
    return (prefix_grad, action_grad, *out)


def solution(mesh):
    rows, sample, cols = P(("dp", "tensor"), None), P("dp", None), P(None, "tensor")
    in_specs = (rows, sample, sample, P(), P()) + (cols,) * 8 + (rows, sample)
    out_specs = (rows, sample) + (P("dp", "tensor"),) * 8
    return jax.shard_map(per_device, mesh=mesh, in_specs=in_specs, out_specs=out_specs, check_vma=False)
```

```python
import functools
import math

import jax
import jax.numpy as jnp
from jax import lax
from jax.experimental import pallas as pl
from jax.experimental.pallas import tpu as pltpu
from jax.sharding import PartitionSpec as P

D = 4608
DA = 2048
H = 32
HD = 128
ROWS = 64
ACT = 48
SLOTS = 8
PREF = SLOTS * ROWS
QW, KW = 512, 256
COLS = 2 * QW + 2 * KW
HALF = COLS // 2
TILE = 256
EPSILON = 1e-06
SOFT_CAP = 50.0
SCALE = 1.0 / math.sqrt(D // H)
MESH = pl.DeviceIdType.MESH
BF16, F32 = jnp.bfloat16, jnp.float32
VMEM = pl.BlockSpec(memory_space=pltpu.VMEM)
ANY = pl.BlockSpec(memory_space=pl.ANY)


def x_step(k):
    return lax.axis_index("dp"), lax.rem(lax.axis_index("tensor") + 2 * k + 8, 8)


def z_step(k):
    return lax.rem(lax.axis_index("dp") + 4 * k + 16, 16), lax.axis_index("tensor")


def y_low():
    t = lax.axis_index("tensor")
    return lax.axis_index("dp"), t + 1 - 2 * lax.rem(t, 2)


def y_high():
    d = lax.axis_index("dp")
    return d + 2 - 4 * lax.rem(lax.div(d, 2), 2), lax.axis_index("tensor")


def sibling():
    d = lax.axis_index("dp")
    return d + 1 - 2 * lax.rem(d, 2), lax.axis_index("tensor")


def slot_order():
    t = lax.axis_index("tensor")
    x, y = lax.div(t, 2), lax.rem(t, 2)

    def at(step, row):
        return 2 * lax.rem(x + step + 4, 4) + row

    return [at(0, y), at(0, 1 - y), at(-1, y), at(1, y), at(2, y), at(-1, 1 - y), at(1, 1 - y), at(2, 1 - y)]


def greet(partners, meanwhile):
    barrier = pltpu.get_barrier_semaphore()
    for device in partners:
        pl.semaphore_signal(barrier, inc=1, device_id=device, device_id_type=MESH)
    meanwhile()
    pl.semaphore_wait(barrier, len(partners))


def remote(src, dst, send, recv, device):
    return pltpu.make_async_remote_copy(
        src_ref=src, dst_ref=dst, send_sem=send, recv_sem=recv, device_id=device, device_id_type=MESH
    )


def norm(rows, gain):
    widened = rows.astype(F32)
    inverse = lax.rsqrt(jnp.mean(widened * widened, -1, keepdims=True) + EPSILON)
    return (widened * inverse * gain).astype(BF16)


def dot_last(a, b):
    return lax.dot_general(a, b, (((1,), (1,)), ((), ())), preferred_element_type=F32)


def soft(key_rows, query_rows):
    t = jnp.tanh(dot_last(key_rows, query_rows) * (SCALE / SOFT_CAP))
    return t, jnp.exp(SOFT_CAP * t)


def attend(h, proj, aproj, seg_row, seg_col, grads, agrads, dk, dv):
    block = 256

    def cols(first, width=HD):
        return pl.ds(pl.multiple_of(first, HD), width)

    key = proj[:, :, cols(QW + HD * h)].reshape(PREF, HD)
    value = proj[:, :, cols(QW + KW + HD * h)].reshape(PREF, HD)
    key_t, value_t = key.T, value.T
    base = HALF * h
    akey = aproj[:, cols(QW + HD * h)]
    avalue = aproj[:, cols(QW + KW + HD * h)]

    def two(first):
        return jnp.concatenate([aproj[:, cols(first + HD * (2 * h + g))] for g in range(2)], 0)

    aq, ado = two(0), two(QW + 2 * KW)
    tp, wp = soft(key, aq)
    ta, wa = soft(akey, aq)
    rate = 1.0 / (jnp.sum(wp, 0, keepdims=True) + jnp.sum(wa, 0, keepdims=True))
    pp, pa = wp * rate, wa * rate
    gp, ga = dot_last(value, ado), dot_last(avalue, ado)
    inner = jnp.sum(pp * gp, 0, keepdims=True) + jnp.sum(pa * ga, 0, keepdims=True)
    sp = (pp * (gp - inner) * (1.0 - tp * tp) * SCALE).astype(BF16)
    sa = (pa * (ga - inner) * (1.0 - ta * ta) * SCALE).astype(BF16)
    pp, pa = pp.astype(BF16), pa.astype(BF16)
    dk[...] = jnp.dot(sp, aq, preferred_element_type=F32)
    dv[...] = jnp.dot(pp, ado, preferred_element_type=F32)
    agrads[:, cols(base + 256)] = jnp.dot(sa, aq, preferred_element_type=F32).astype(BF16)
    agrads[:, cols(base + 384)] = jnp.dot(pa, ado, preferred_element_type=F32).astype(BF16)
    adq = (jnp.dot(key_t, sp, preferred_element_type=F32) + jnp.dot(akey.T, sa, preferred_element_type=F32)).T
    aat = (jnp.dot(value_t, pp, preferred_element_type=F32) + jnp.dot(avalue.T, pa, preferred_element_type=F32)).T
    for g in range(2):
        agrads[:, cols(base + HD * g)] = adq[ACT * g : ACT * (g + 1)].astype(BF16)
        agrads[:, cols(base + 512 + HD * g)] = aat[ACT * g : ACT * (g + 1)].astype(BF16)

    for g in range(2):
        for b in range(PREF // block):
            rows = slice(b * block, (b + 1) * block)
            slots = slice(b * block // ROWS, (b + 1) * block // ROWS)
            first = HD * (2 * h + g)
            query = proj[slots, :, cols(first)].reshape(block, HD)
            dout = proj[slots, :, cols(QW + 2 * KW + first)].reshape(block, HD)
            t, w = soft(key, query)
            w = jnp.where(seg_col <= seg_row[:, rows], w, 0.0)
            p = w * (1.0 / jnp.sum(w, 0, keepdims=True))
            gp = dot_last(value, dout)
            inner = jnp.sum(p * gp, 0, keepdims=True)
            s = (p * (gp - inner) * (1.0 - t * t) * SCALE).astype(BF16)
            p = p.astype(BF16)
            dk[...] += jnp.dot(s, query, preferred_element_type=F32)
            dv[...] += jnp.dot(p, dout, preferred_element_type=F32)
            dq = jnp.dot(key_t, s, preferred_element_type=F32).T
            at = jnp.dot(value_t, p, preferred_element_type=F32).T
            grads[rows, cols(base + HD * g)] = dq.astype(BF16)
            grads[rows, cols(base + 512 + HD * g)] = at.astype(BF16)
    grads[:, cols(base + 256)] = dk[...].astype(BF16)
    grads[:, cols(base + 384)] = dv[...].astype(BF16)


def gather_kernel(
    pin, cot, gain, ain, acot, again, seg, wq, wk, wv, wo, aq, ak, av, ao,
    grads, agrads, s_grads, sa_grads, g_norm, g_cot, s_norm, s_cot, a_norm, sa_norm, sa_cot,
    norm_v, cot_v, w_v, aw_v, proj, aproj, dk, dv,
    send, recv, sib_send, sib_recv, local, w_sem, act_send, act_recv,
):
    weights = []
    for i, (ref, first) in enumerate(((aq, 0), (ak, QW), (av, QW + KW), (ao, QW + 2 * KW))):
        weights.append(pltpu.make_async_copy(ref, aw_v.at[:, pl.ds(first, ref.shape[1])], w_sem.at[i]))
    for i, (ref, first) in enumerate(((wq, 0), (wk, QW), (wv, QW + KW), (wo, QW + 2 * KW))):
        weights.append(pltpu.make_async_copy(ref, w_v.at[:, pl.ds(first, ref.shape[1])], w_sem.at[4 + i]))
    for copy in weights:
        copy.start()
    left, right, across, twin = x_step(-1), x_step(1), y_low(), sibling()

    def own_rows():
        cot_v[0] = cot[...]
        norm_v[0] = norm(pin[...], gain[...])

    greet((left, right, across, twin), own_rows)

    arrays = ((norm_v, g_norm, s_norm), (cot_v, g_cot, s_cot))

    def hop(a, src, dst, device):
        held = arrays[a][0]
        return remote(held.at[src], held.at[dst], send.at[a, dst], recv.at[a, dst], device)

    hops = [
        {1: hop(a, 0, 1, across), 2: hop(a, 0, 2, right), 3: hop(a, 0, 3, left),
         4: hop(a, 2, 4, right) if a == 0 else hop(a, 3, 4, left),
         5: hop(a, 1, 5, right), 6: hop(a, 1, 6, left), 7: hop(a, 4, 7, across)}
        for a in range(2)
    ]
    twins = [
        [remote(held.at[s], far.at[s], sib_send.at[a, s], sib_recv.at[a, s], twin) for s in range(SLOTS)]
        for a, (held, _, far) in enumerate(arrays)
    ]
    stores = [
        [pltpu.make_async_copy(held.at[s], near.at[s], local.at[a, s]) for s in range(SLOTS)]
        for a, (held, near, _) in enumerate(arrays)
    ]

    def spread(a, s):
        twins[a][s].start()
        stores[a][s].start()

    right_of = (hops[0][2], hops[1][2])
    left_of = (hops[0][3], hops[1][3])
    right_of[0].start()
    left_of[1].start()
    for a in range(2):
        hops[a][1].start()
    spread(1, 0)
    spread(0, 0)

    a_norm[...] = norm(ain[...], again[...])
    act_twins = [
        remote(a_norm, sa_norm, act_send.at[0], act_recv.at[0], twin),
        remote(acot, sa_cot, act_send.at[1], act_recv.at[1], twin),
    ]
    for copy in act_twins:
        copy.start()
    for copy in weights[:4]:
        copy.wait()

    def act_project(rows, first):
        def step(j, carry):
            cols = pl.ds(pl.multiple_of(j * TILE, TILE), TILE)
            aproj[:, cols] = jnp.dot(rows[...], aw_v[:, cols], preferred_element_type=F32).astype(BF16)
            return carry

        lax.fori_loop(first, first + (4 if first == 0 else 2), step, 0)

    act_project(a_norm, 0)
    act_project(acot, 4)

    def project(held, low, high, first):
        def step(j, carry):
            cols = pl.ds(pl.multiple_of(j * TILE, TILE), TILE)
            rows = held[low:high].reshape((high - low) * ROWS, D)
            out = jnp.dot(rows, w_v[:, cols], preferred_element_type=F32).astype(BF16)
            proj[low:high, :, cols] = out.reshape(high - low, ROWS, TILE)
            return carry

        lax.fori_loop(first, first + (4 if first == 0 else 2), step, 0)

    right_of[0].wait_send()
    right_of[1].start()
    left_of[1].wait_send()
    left_of[0].start()
    hops[0][2].wait_recv()
    hops[0][4].start()
    hops[1][3].wait_recv()
    hops[1][4].start()
    spread(0, 2)
    spread(1, 3)
    for copy in weights[4:]:
        copy.wait()
    for a in range(2):
        hops[a][1].wait_recv()
        spread(a, 1)
    hops[0][4].wait_send()
    hops[0][5].start()
    hops[1][4].wait_send()
    hops[0][6].start()
    for a in range(2):
        hops[a][4].wait_recv()
        hops[a][7].start()
        spread(a, 4)
    right_of[1].wait_send()
    left_of[0].wait_send()
    hops[1][2].wait_recv()
    hops[0][3].wait_recv()
    spread(1, 2)
    spread(0, 3)
    project(norm_v, 0, 4, 0)
    hops[0][5].wait_send()
    hops[1][5].start()
    hops[0][6].wait_send()
    hops[1][6].start()
    project(cot_v, 0, 4, 4)
    for a, first in ((0, 0), (1, 4)):
        for s in (5, 6, 7):
            hops[a][s].wait_recv()
            spread(a, s)
        project(arrays[a][0], 4, 8, first)

    core = lax.rem(lax.axis_index("dp"), 2)
    seg_row = jnp.concatenate([seg[pl.ds(s, 1), :] for s in slot_order()], 1).astype(F32)
    seg_col = jnp.broadcast_to(seg_row, (8, PREF)).T[:, 0:1]
    attend(1 - core, proj, aproj, seg_row, seg_col, grads, agrads, dk, dv)
    theirs = pl.ds(pl.multiple_of((1 - core) * HALF, HALF), HALF)
    act_twins += [
        remote(grads.at[:, theirs], s_grads, act_send.at[2], act_recv.at[2], twin),
        remote(agrads.at[:, theirs], sa_grads, act_send.at[3], act_recv.at[3], twin),
    ]
    for copy in act_twins[2:]:
        copy.start()
    attend(core, proj, aproj, seg_row, seg_col, grads, agrads, dk, dv)
    for a in range(2):
        hops[a][1].wait_send()
        hops[a][7].wait_send()
        for s in range(SLOTS):
            twins[a][s].wait()
            stores[a][s].wait()
    for s in (5, 6):
        hops[1][s].wait_send()
    for copy in act_twins:
        copy.wait()


def gather_and_attend(pin, cot, gain, ain, acot, again, seg, *weights):
    rows = jax.ShapeDtypeStruct((SLOTS, ROWS, D), BF16)
    acts = jax.ShapeDtypeStruct((ACT, DA), BF16)
    dma = pltpu.SemaphoreType.DMA
    return pl.pallas_call(
        gather_kernel,
        out_shape=(
            jax.ShapeDtypeStruct((PREF, COLS), BF16), jax.ShapeDtypeStruct((ACT, COLS), BF16),
            jax.ShapeDtypeStruct((PREF, HALF), BF16), jax.ShapeDtypeStruct((ACT, HALF), BF16),
            rows, rows, rows, rows, acts, acts, acts,
        ),
        in_specs=[VMEM] * 7 + [ANY] * 8,
        out_specs=(VMEM, VMEM, ANY, ANY, ANY, ANY, ANY, ANY, VMEM, ANY, ANY),
        scratch_shapes=[
            pltpu.VMEM((SLOTS, ROWS, D), BF16), pltpu.VMEM((SLOTS, ROWS, D), BF16),
            pltpu.VMEM((D, COLS), BF16), pltpu.VMEM((DA, COLS), BF16),
            pltpu.VMEM((SLOTS, ROWS, COLS), BF16), pltpu.VMEM((ACT, COLS), BF16),
            pltpu.VMEM((PREF, HD), F32), pltpu.VMEM((PREF, HD), F32),
            dma((2, SLOTS)), dma((2, SLOTS)), dma((2, SLOTS)), dma((2, SLOTS)), dma((2, SLOTS)),
            dma((8,)), dma((4,)), dma((4,)),
        ],
        compiler_params=pltpu.CompilerParams(
            collective_id=0, has_side_effects=True, vmem_limit_bytes=60 << 20
        ),
        name="gather_and_attend",
    )(pin, cot, gain[None, :], ain, acot, again[None, :], seg, *weights)


SHARE = 416
PRE, ACTS = 288, 128
Z_PRE, Z_ACT = 4 * PRE, 4 * ACTS
LHS_TILE = 384
UP_TILE = 384
ACT_TILE = 512
HALF_D = D // 2


class Link:
    def __init__(self, window):
        self.window, self.flying = window, []

    def start(self, copy):
        if len(self.flying) == self.window:
            self.flying.pop(0).wait_send()
        copy.start()
        self.flying.append(copy)

    def drain(self):
        for copy in self.flying:
            copy.wait_send()


def add(*terms):
    total = terms[0].astype(F32)
    for term in terms[1:]:
        total = total + term.astype(F32)
    return total


def norm_back(rows, gain, upstream):
    widened = rows.astype(F32)
    inverse = lax.rsqrt(jnp.mean(widened * widened, -1, keepdims=True) + EPSILON)
    normed = widened * inverse
    scaled = upstream * gain
    return (inverse * (scaled - normed * jnp.mean(scaled * normed, -1, keepdims=True))).astype(BF16)


def sum_kernel(
    g_norm, g_cot, s_norm, s_cot, s_grads, a_norm, acot, sa_norm, sa_cot, grads, agrads, sa_grads, pin, gain, ain, again,
    wq, wk, wv, aq, ak, av,
    pgrad, agrad, final,
    left_v, act_v, right_v, aright_v, w_v, part, z1_v, z2_v, h1_v, h2_v, y0_v, y_v, done_v, up_v, u1_v, u2_v, uy_v, aup_v, ay_v, ax_v,
    load_sem, w_sem, ex_sem, z1_send, z1_recv, z2_send, z2_recv, h1_send, h1_recv, h2_send, h2_recv, y0_send, y0_recv, y_send, y_recv, f_send, f_recv, f_local,
    u1_send, u1_recv, u2_send, u2_recv, uy_send, uy_recv, ay_send, ay_recv, ax_send, ax_recv,
):
    d = lax.axis_index("dp")
    z, yh, core = lax.div(d, 4), lax.rem(lax.div(d, 2), 2), lax.rem(d, 2)
    steps = (2, 1, -1, 0)
    z_of = [lax.rem(z + s + 4, 4) for s in steps]

    loads = {}
    for r in range(4):
        for a, pair in enumerate(((g_norm, s_norm), (g_cot, s_cot))):
            cols = pl.ds(pl.multiple_of(z_of[r] * Z_PRE, 128), Z_PRE)
            loads[a, r] = [
                pltpu.make_async_copy(
                    ref.at[:, cols], left_v.at[a, r, pl.ds(PREF * i, PREF)], load_sem.at[a, r, i])
                for i, ref in enumerate(pair)
            ]
    def w_copies(refs, tile, t):
        slot = lax.rem(t, 3)
        rows = pl.ds(pl.multiple_of(t * tile, tile), tile)
        copies = []
        for h in range(2):
            for j, (ref, width, first) in enumerate(zip(refs, (256, 128, 128), (0, 256, 384))):
                copies.append(pltpu.make_async_copy(
                    ref.at[rows, pl.ds(width * h, width)],
                    w_v.at[slot, pl.ds(0, tile), pl.ds(512 * h + first, width)],
                    w_sem.at[slot, 3 * h + j]))
        return copies

    def prime(refs, tile):
        for t in range(2):
            for copy in w_copies(refs, tile, t):
                copy.start()

    prime((aq, ak, av), ACT_TILE)
    z_right, z_left, across, twin = z_step(1), z_step(-1), y_high(), sibling()
    x_right, x_left, x_far, y_near = x_step(1), x_step(-1), x_step(2), y_low()
    mine = pl.ds(pl.multiple_of(core * HALF, HALF), HALF)
    twin_half = pltpu.make_async_copy(s_grads, right_v.at[pl.ds(PREF, PREF)], ex_sem.at[0])
    twin_half.start()
    for key in ((0, 0), (0, 1), (0, 2), (0, 3)):
        for copy in loads[key]:
            copy.start()
    right_v[0:PREF] = grads[:, mine]
    aright_v[0:ACT] = agrads[:, mine]
    aright_v[ACT : 2 * ACT] = sa_grads[...]
    act_v[0, 0:ACT] = a_norm[...]
    act_v[0, ACT : 2 * ACT] = sa_norm[...]
    act_v[1, 0:ACT] = acot[...]
    act_v[1, ACT : 2 * ACT] = sa_cot[...]
    twin_half.wait()

    loaded = set()

    def weight_grad(g, r):
        a = 0 if g < 2 else 1
        if (a, r) not in loaded:
            loaded.add((a, r))
            for copy in loads[a, r]:
                copy.wait()
        cols = slice(256 * g, 256 * (g + 1))
        for t in range(Z_PRE // LHS_TILE):
            low, high = t * LHS_TILE, (t + 1) * LHS_TILE
            out = lax.dot_general(
                left_v[a, r, :, low:high], right_v[:, cols], (((0,), (0,)), ((), ())), preferred_element_type=F32
            ).astype(BF16)
            for share in range(4):
                first, last = max(low, PRE * share), min(high, PRE * (share + 1))
                if first < last:
                    part[g, r, share // 2, share % 2, first - PRE * share : last - PRE * share] = (
                        out[first - low : last - low])
        out = lax.dot_general(
            act_v[a, :, pl.ds(pl.multiple_of(z_of[r] * Z_ACT, Z_ACT), Z_ACT)], aright_v[:, cols],
            (((0,), (0,)), ((), ())), preferred_element_type=F32,
        ).astype(BF16)
        for share in range(4):
            part[g, r, share // 2, share % 2, PRE:SHARE] = out[ACTS * share : ACTS * (share + 1)]

    sides = (z_right, z_left)
    z1 = {g: [
        remote(part.at[g, 0, i], z1_v.at[g - 1, i], z1_send.at[g - 1, i], z1_recv.at[g - 1, i], sides[i])
        for i in range(2)] for g in (1, 2)}
    z2 = {g: [[
        remote(part.at[g, 1 + i, y], z2_v.at[g - 1, i, y], z2_send.at[g - 1, i, y], z2_recv.at[g - 1, i, y], sides[i])
        for y in range(2)] for i in range(2)] for g in (1, 2)}
    ys = {g: remote(part.at[g, 3, 1 - yh], y_v.at[g - 1], y_send.at[g - 1], y_recv.at[g - 1], across) for g in (1, 2)}
    y0 = [remote(part.at[0, r, 1 - yh], y0_v.at[r], y0_send.at[r], y0_recv.at[r], across) for r in range(4)]
    h1 = [remote(part.at[0, 0, yh, i], h1_v.at[i], h1_send.at[i], h1_recv.at[i], sides[i]) for i in range(2)]
    h2 = [[
        remote(part.at[0, 1 + i, yh, c], h2_v.at[i, c], h2_send.at[i, c], h2_recv.at[i, c], sides[i])
        for c in range(2)] for i in range(2)]
    outs = [
        remote(done_v.at[g, 1 - core], final.at[core, g], f_send.at[g], f_recv.at[g], twin) for g in range(3)
    ]
    kept = [pltpu.make_async_copy(done_v.at[g, core], final.at[core, g], f_local.at[g]) for g in range(3)]
    z_links, y_link = (Link(2), Link(2)), Link(2)

    def z_first(g, compute=True):
        if compute:
            weight_grad(g, 0)
        for i in range(2):
            z_links[i].start(z1[g][i])

    def z_raw(g):
        for i in range(2):
            weight_grad(g, 1 + i)
            z_links[i].start(z2[g][i][1 - i])

    def z_second(g):
        for i in range(2):
            z1[g][i].wait_recv()
            part[g, 1 + i, i] = add(part[g, 1 + i, i], z1_v[g - 1, i]).astype(BF16)
            z_links[i].start(z2[g][i][i])

    def y_last(g):
        for i in range(2):
            for y in range(2):
                z2[g][i][y].wait_recv()
        y = 1 - yh
        part[g, 3, y] = add(part[g, 3, y], z2_v[g - 1, 0, y], z2_v[g - 1, 1, y]).astype(BF16)
        y_link.start(ys[g])

    def hand_over(g):
        outs[g].start()
        kept[g].start()

    def finish(g):
        ys[g].wait_recv()
        done_v[g] = add(part[g, 3, yh], z2_v[g - 1, 0, yh], z2_v[g - 1, 1, yh], y_v[g - 1]).astype(BF16)
        hand_over(g)

    def y_first(r):
        weight_grad(0, r)
        y_link.start(y0[r])

    def y_add(r):
        y0[r].wait_recv()
        part[0, r, yh] = add(part[0, r, yh], y0_v[r]).astype(BF16)

    def h_first():
        y_add(0)
        for i in range(2):
            z_links[i].start(h1[i])

    def h_raw():
        for i in range(2):
            y_add(1 + i)
            z_links[i].start(h2[i][1 - i])

    def h_second():
        for i in range(2):
            h1[i].wait_recv()
            part[0, 1 + i, yh, i] = add(part[0, 1 + i, yh, i], h1_v[i]).astype(BF16)
            z_links[i].start(h2[i][i])

    def h_finish():
        y_add(3)
        for i in range(2):
            for c in range(2):
                h2[i][c].wait_recv()
        done_v[0] = add(part[0, 3, yh], h2_v[0], h2_v[1]).astype(BF16)
        hand_over(0)

    def up_loop(refs, tile, first, last, count, use):
        def step(t, carry):
            @pl.when(t + 2 < count)
            def _():
                for copy in w_copies(refs, tile, t + 2):
                    copy.start()

            for copy in w_copies(refs, tile, t):
                copy.wait()
            use(t, lax.rem(t, 3))
            return carry

        lax.fori_loop(first, last, step, 0)

    def through(cots, slot, tile):
        return dot_last(cots[:, 0:512], w_v[slot, 0:tile, 0:512]) + dot_last(
            cots[:, HALF : HALF + 512], w_v[slot, 0:tile, 512:1024])

    def use_pre(t, slot):
        cols = pl.ds(pl.multiple_of(t * UP_TILE, UP_TILE), UP_TILE)
        up_v[:, :, cols] = through(grads, slot, UP_TILE).astype(BF16).reshape(SLOTS, ROWS, UP_TILE)

    def use_act(t, slot):
        cols = pl.ds(pl.multiple_of(t * ACT_TILE, ACT_TILE), ACT_TILE)
        aup_v[:, cols] = through(agrads, slot, ACT_TILE).astype(BF16)

    def act_loop():
        up_loop((aq, ak, av), ACT_TILE, 0, DA // ACT_TILE, DA // ACT_TILE, use_act)

    def pre_loop(half):
        count = D // UP_TILE
        up_loop((wq, wk, wv), UP_TILE, half * count // 2, (half + 1) * count // 2, count, use_pre)

    u1, u2, uy = [], [], []
    for p in range(2):
        cols = pl.ds(HALF_D * p, HALF_D)
        u1.append([
            remote(up_v.at[s, :, cols], u1_v.at[i, :, cols], u1_send.at[p, i], u1_recv.at[p, i], device)
            for i, (s, device) in enumerate(((4, x_right), (7, x_left)))])
        u2.append([
            remote(up_v.at[s, :, cols], u2_v.at[i, :, cols], u2_send.at[p, i], u2_recv.at[p, i], device)
            for i, (s, device) in enumerate(((3, x_right), (6, x_right), (2, x_left), (5, x_left)))])
        uy.append(remote(up_v.at[1, :, cols], uy_v.at[:, cols], uy_send.at[p], uy_recv.at[p], y_near))
    ay = remote(aup_v, ay_v, ay_send.at[0], ay_recv.at[0], y_near)
    ax = [
        remote(ax_v.at[0], ax_v.at[1 + i], ax_send.at[i], ax_recv.at[i], device)
        for i, device in enumerate((x_right, x_left, x_far))
    ]

    def up_step():
        ay.wait_recv()
        ax_v[0] = add(aup_v[...], ay_v[...]).astype(BF16)
        for copy in ax:
            copy.start()

    def up_start(p):
        pre_loop(p)
        for copy in (u1[p][0], u1[p][1], u2[p][1], u2[p][2]):
            copy.start()

    def up_add(p):
        cols = slice(HALF_D * p, HALF_D * (p + 1))
        for i, s in ((0, 3), (1, 5)):
            u1[p][i].wait_recv()
            up_v[s, :, cols] = add(up_v[s, :, cols], u1_v[i, :, cols]).astype(BF16)
        u2[p][0].start()
        u2[p][3].start()

    def up_last(p):
        cols = slice(HALF_D * p, HALF_D * (p + 1))
        for copy in u2[p]:
            copy.wait_recv()
        up_v[1, :, cols] = add(up_v[1, :, cols], u2_v[1, :, cols], u2_v[3, :, cols]).astype(BF16)
        uy[p].start()

    def before():
        act_loop()
        weight_grad(1, 0)

    greet((z_right, z_left, across, twin, x_right, x_left, x_far, y_near), before)
    z_first(1, compute=False)
    ay.start()
    prime((wq, wk, wv), UP_TILE)
    y_first(0)
    up_step()
    up_start(0)
    z_raw(1)
    up_start(1)
    for key in ((1, 0), (1, 1), (1, 2), (1, 3)):
        for copy in loads[key]:
            copy.start()
    y_first(1)
    z_first(2)
    z_second(1)
    y_first(2)
    up_add(0)
    y_first(3)
    up_add(1)
    z_raw(2)
    weight_grad(1, 3)
    y_last(1)
    weight_grad(2, 3)
    up_last(0)
    z_second(2)
    up_last(1)
    h_first()
    for copy in ax:
        copy.wait_recv()
    agrad[...] = norm_back(ain[...], again[...], add(ax_v[0], ax_v[3]) + add(ax_v[1], ax_v[2]))
    finish(1)
    h_raw()
    y_last(2)
    h_second()
    for copy in uy:
        copy.wait_recv()
    pgrad[...] = norm_back(pin[...], gain[...], add(up_v[0], u2_v[0], u2_v[2], uy_v[...]))
    finish(2)
    h_finish()

    for copy in (*u1[0], *u1[1], *u2[0], *u2[1], *uy, ay, *ax):
        copy.wait_send()
    for link in (*z_links, y_link):
        link.drain()
    for g in range(3):
        outs[g].wait()
        kept[g].wait()


def sum_everything(g_norm, g_cot, s_norm, s_cot, *rest):
    wide = tuple(m.reshape(PREF, D) for m in (g_norm, g_cot, s_norm, s_cot))
    dma = pltpu.SemaphoreType.DMA
    share = (2, SHARE, 256)
    row = (ROWS, D)

    def held(*shape):
        return pltpu.VMEM(shape, BF16)

    return pl.pallas_call(
        sum_kernel,
        out_shape=(
            jax.ShapeDtypeStruct(row, BF16), jax.ShapeDtypeStruct((ACT, DA), BF16),
            jax.ShapeDtypeStruct((2, 3, SHARE, 256), BF16),
        ),
        in_specs=[ANY] * 5 + [VMEM] * 11 + [ANY] * 6,
        out_specs=(VMEM, VMEM, ANY),
        scratch_shapes=[
            held(2, 4, 2 * PREF, Z_PRE), held(2, 2 * ACT, DA), held(2 * PREF, HALF), held(2 * ACT, HALF),
            held(3, ACT_TILE, 1024), held(3, 4, 2, *share), held(2, 2, *share), held(2, 2, 2, *share),
            held(*share), held(2, *share), held(4, *share), held(2, *share), held(3, *share), held(SLOTS, *row), held(2, *row), held(4, *row), held(*row),
            held(ACT, DA), held(ACT, DA), held(4, ACT, DA),
            dma((2, 4, 2)), dma((3, 6)), dma((1,)), dma((2, 2)), dma((2, 2)), dma((2, 2, 2)), dma((2, 2, 2)),
            dma((2,)), dma((2,)), dma((2, 2)), dma((2, 2)), dma((4,)), dma((4,)),
            dma((2,)), dma((2,)), dma((3,)), dma((3,)), dma((3,)),
            dma((2, 2)), dma((2, 2)), dma((2, 4)), dma((2, 4)), dma((2,)), dma((2,)),
            dma((1,)), dma((1,)), dma((3,)), dma((3,)),
        ],
        compiler_params=pltpu.CompilerParams(
            collective_id=1, has_side_effects=True, vmem_limit_bytes=62 << 20
        ),
        name="sum_everything",
    )(*wide, *rest)


def assemble_kernel(final, pgrad, agrad, *outs):
    outs[0][...] = pgrad[...]
    outs[1][...] = agrad[...]
    at = 2
    for rows in (slice(0, PRE), slice(PRE, SHARE)):
        for g, first, width in ((0, 0, 256), (1, 0, 128), (1, 128, 128), (2, 0, 256)):
            for h in range(2):
                outs[at][:, width * h : width * (h + 1)] = final[h, g, rows, first : first + width]
            at += 1


def assemble(final, pgrad, agrad):
    widths = (QW, KW, KW, QW)
    return pl.pallas_call(
        assemble_kernel,
        out_shape=tuple(
            [jax.ShapeDtypeStruct(pgrad.shape, BF16), jax.ShapeDtypeStruct(agrad.shape, BF16)]
            + [jax.ShapeDtypeStruct((rows, w), BF16) for rows in (PRE, ACTS) for w in widths]),
        in_specs=[VMEM] * 3,
        out_specs=(VMEM,) * 10,
        compiler_params=pltpu.CompilerParams(vmem_limit_bytes=32 << 20),
        name="assemble",
    )(final, pgrad, agrad)


def per_device(prefix_in, action_in, segment_ids, gain_prefix, gain_action, query_prefix, key_prefix, value_prefix,
               out_prefix, query_action, key_action, value_action, out_action, cot_prefix, cot_action):
    grads, agrads, s_grads, sa_grads, g_norm, g_cot, s_norm, s_cot, a_norm, sa_norm, sa_cot = gather_and_attend(
        prefix_in, cot_prefix, gain_prefix, action_in, cot_action, gain_action, segment_ids.reshape(SLOTS, ROWS),
        query_prefix, key_prefix, value_prefix, out_prefix, query_action, key_action, value_action, out_action)
    prefix_grad, action_grad, final = sum_everything(
        g_norm, g_cot, s_norm, s_cot, s_grads, a_norm, cot_action, sa_norm, sa_cot, grads, agrads, sa_grads,
        prefix_in, gain_prefix[None, :], action_in, gain_action[None, :],
        query_prefix, key_prefix, value_prefix, query_action, key_action, value_action)
    return assemble(final, prefix_grad, action_grad)


def solution(mesh):
    rows, sample, cols = P(("dp", "tensor"), None), P("dp", None), P(None, "tensor")
    in_specs = (rows, sample, sample, P(), P()) + (cols,) * 8 + (rows, sample)
    out_specs = (rows, sample) + (P("dp", "tensor"),) * 8
    return jax.shard_map(per_device, mesh=mesh, in_specs=in_specs, out_specs=out_specs, check_vma=False)
```

```python
import functools
import math

import jax
import jax.numpy as jnp
from jax import lax
from jax.experimental import pallas as pl
from jax.experimental.pallas import tpu as pltpu
from jax.sharding import PartitionSpec as P

D = 4608
DA = 2048
H = 32
HD = 128
ROWS = 64
ACT = 48
SLOTS = 8
PREF = SLOTS * ROWS
QW, KW = 512, 256
COLS = 2 * QW + 2 * KW
HALF = COLS // 2
TILE = 256
EPSILON = 1e-06
SOFT_CAP = 50.0
SCALE = 1.0 / math.sqrt(D // H)
MESH = pl.DeviceIdType.MESH
BF16, F32 = jnp.bfloat16, jnp.float32
VMEM = pl.BlockSpec(memory_space=pltpu.VMEM)
ANY = pl.BlockSpec(memory_space=pl.ANY)


def x_step(k):
    return lax.axis_index("dp"), lax.rem(lax.axis_index("tensor") + 2 * k + 8, 8)


def z_step(k):
    return lax.rem(lax.axis_index("dp") + 4 * k + 16, 16), lax.axis_index("tensor")


def y_low():
    t = lax.axis_index("tensor")
    return lax.axis_index("dp"), t + 1 - 2 * lax.rem(t, 2)


def y_high():
    d = lax.axis_index("dp")
    return d + 2 - 4 * lax.rem(lax.div(d, 2), 2), lax.axis_index("tensor")


def sibling():
    d = lax.axis_index("dp")
    return d + 1 - 2 * lax.rem(d, 2), lax.axis_index("tensor")


def slot_order():
    t = lax.axis_index("tensor")
    x, y = lax.div(t, 2), lax.rem(t, 2)

    def at(step, row):
        return 2 * lax.rem(x + step + 4, 4) + row

    return [at(0, y), at(0, 1 - y), at(-1, y), at(1, y), at(2, y), at(-1, 1 - y), at(1, 1 - y), at(2, 1 - y)]


def greet(partners, meanwhile):
    barrier = pltpu.get_barrier_semaphore()
    for device in partners:
        pl.semaphore_signal(barrier, inc=1, device_id=device, device_id_type=MESH)
    meanwhile()
    pl.semaphore_wait(barrier, len(partners))


def remote(src, dst, send, recv, device):
    return pltpu.make_async_remote_copy(
        src_ref=src, dst_ref=dst, send_sem=send, recv_sem=recv, device_id=device, device_id_type=MESH
    )


def norm(rows, gain):
    widened = rows.astype(F32)
    inverse = lax.rsqrt(jnp.mean(widened * widened, -1, keepdims=True) + EPSILON)
    return (widened * inverse * gain).astype(BF16)


def dot_last(a, b):
    return lax.dot_general(a, b, (((1,), (1,)), ((), ())), preferred_element_type=F32)


def soft(key_rows, query_rows):
    t = jnp.tanh(dot_last(key_rows, query_rows) * (SCALE / SOFT_CAP))
    return t, jnp.exp(SOFT_CAP * t)


def attend(h, proj, aproj, seg_row, seg_col, grads, agrads, dk, dv):
    block = 256

    def cols(first, width=HD):
        return pl.ds(pl.multiple_of(first, HD), width)

    key = proj[:, :, cols(QW + HD * h)].reshape(PREF, HD)
    value = proj[:, :, cols(QW + KW + HD * h)].reshape(PREF, HD)
    key_t, value_t = key.T, value.T
    base = HALF * h
    akey = aproj[:, cols(QW + HD * h)]
    avalue = aproj[:, cols(QW + KW + HD * h)]

    def two(first):
        return jnp.concatenate([aproj[:, cols(first + HD * (2 * h + g))] for g in range(2)], 0)

    aq, ado = two(0), two(QW + 2 * KW)
    tp, wp = soft(key, aq)
    ta, wa = soft(akey, aq)
    rate = 1.0 / (jnp.sum(wp, 0, keepdims=True) + jnp.sum(wa, 0, keepdims=True))
    pp, pa = wp * rate, wa * rate
    gp, ga = dot_last(value, ado), dot_last(avalue, ado)
    inner = jnp.sum(pp * gp, 0, keepdims=True) + jnp.sum(pa * ga, 0, keepdims=True)
    sp = (pp * (gp - inner) * (1.0 - tp * tp) * SCALE).astype(BF16)
    sa = (pa * (ga - inner) * (1.0 - ta * ta) * SCALE).astype(BF16)
    pp, pa = pp.astype(BF16), pa.astype(BF16)
    dk[...] = jnp.dot(sp, aq, preferred_element_type=F32)
    dv[...] = jnp.dot(pp, ado, preferred_element_type=F32)
    agrads[:, cols(base + 256)] = jnp.dot(sa, aq, preferred_element_type=F32).astype(BF16)
    agrads[:, cols(base + 384)] = jnp.dot(pa, ado, preferred_element_type=F32).astype(BF16)
    adq = (jnp.dot(key_t, sp, preferred_element_type=F32) + jnp.dot(akey.T, sa, preferred_element_type=F32)).T
    aat = (jnp.dot(value_t, pp, preferred_element_type=F32) + jnp.dot(avalue.T, pa, preferred_element_type=F32)).T
    for g in range(2):
        agrads[:, cols(base + HD * g)] = adq[ACT * g : ACT * (g + 1)].astype(BF16)
        agrads[:, cols(base + 512 + HD * g)] = aat[ACT * g : ACT * (g + 1)].astype(BF16)

    for g in range(2):
        for b in range(PREF // block):
            rows = slice(b * block, (b + 1) * block)
            slots = slice(b * block // ROWS, (b + 1) * block // ROWS)
            first = HD * (2 * h + g)
            query = proj[slots, :, cols(first)].reshape(block, HD)
            dout = proj[slots, :, cols(QW + 2 * KW + first)].reshape(block, HD)
            t, w = soft(key, query)
            w = jnp.where(seg_col <= seg_row[:, rows], w, 0.0)
            p = w * (1.0 / jnp.sum(w, 0, keepdims=True))
            gp = dot_last(value, dout)
            inner = jnp.sum(p * gp, 0, keepdims=True)
            s = (p * (gp - inner) * (1.0 - t * t) * SCALE).astype(BF16)
            p = p.astype(BF16)
            dk[...] += jnp.dot(s, query, preferred_element_type=F32)
            dv[...] += jnp.dot(p, dout, preferred_element_type=F32)
            dq = jnp.dot(key_t, s, preferred_element_type=F32).T
            at = jnp.dot(value_t, p, preferred_element_type=F32).T
            grads[rows, cols(base + HD * g)] = dq.astype(BF16)
            grads[rows, cols(base + 512 + HD * g)] = at.astype(BF16)
    grads[:, cols(base + 256)] = dk[...].astype(BF16)
    grads[:, cols(base + 384)] = dv[...].astype(BF16)


def gather_kernel(
    pin, cot, gain, ain, acot, again, seg, wq, wk, wv, wo, aq, ak, av, ao,
    grads, agrads, s_grads, sa_grads, g_norm, g_cot, s_norm, s_cot, a_norm, sa_norm, sa_cot,
    norm_v, cot_v, w_v, aw_v, proj, aproj, dk, dv, seg_v,
    send, recv, sib_send, sib_recv, local, w_sem, act_send, act_recv,
):
    weights = []
    for i, (ref, first) in enumerate(((aq, 0), (ak, QW), (av, QW + KW), (ao, QW + 2 * KW))):
        weights.append(pltpu.make_async_copy(ref, aw_v.at[:, pl.ds(first, ref.shape[1])], w_sem.at[i]))
    for i, (ref, first) in enumerate(((wq, 0), (wk, QW), (wv, QW + KW), (wo, QW + 2 * KW))):
        weights.append(pltpu.make_async_copy(ref, w_v.at[:, pl.ds(first, ref.shape[1])], w_sem.at[4 + i]))
    for copy in weights:
        copy.start()
    left, right, across, twin = x_step(-1), x_step(1), y_low(), sibling()

    def own_rows():
        cot_v[0] = cot[...]
        norm_v[0] = norm(pin[...], gain[...].reshape(1, D))

    greet((left, right, across, twin), own_rows)

    arrays = ((norm_v, g_norm, s_norm), (cot_v, g_cot, s_cot))

    def hop(a, src, dst, device):
        held = arrays[a][0]
        return remote(held.at[src], held.at[dst], send.at[a, dst], recv.at[a, dst], device)

    hops = [
        {1: hop(a, 0, 1, across), 2: hop(a, 0, 2, right), 3: hop(a, 0, 3, left),
         4: hop(a, 2, 4, right) if a == 0 else hop(a, 3, 4, left),
         5: hop(a, 1, 5, right), 6: hop(a, 1, 6, left), 7: hop(a, 4, 7, across)}
        for a in range(2)
    ]
    twins = [
        [remote(held.at[s], far.at[s], sib_send.at[a, s], sib_recv.at[a, s], twin) for s in range(SLOTS)]
        for a, (held, _, far) in enumerate(arrays)
    ]
    stores = [
        [pltpu.make_async_copy(held.at[s], near.at[s], local.at[a, s]) for s in range(SLOTS)]
        for a, (held, near, _) in enumerate(arrays)
    ]

    def spread(a, s):
        twins[a][s].start()
        stores[a][s].start()

    right_of = (hops[0][2], hops[1][2])
    left_of = (hops[0][3], hops[1][3])
    right_of[0].start()
    left_of[1].start()
    for a in range(2):
        hops[a][1].start()
    spread(1, 0)
    spread(0, 0)

    a_norm[...] = norm(ain[...], again[...].reshape(1, DA))
    act_twins = [
        remote(a_norm, sa_norm, act_send.at[0], act_recv.at[0], twin),
        remote(acot, sa_cot, act_send.at[1], act_recv.at[1], twin),
    ]
    for copy in act_twins:
        copy.start()
    for copy in weights[:4]:
        copy.wait()

    def act_project(rows, first):
        def step(j, carry):
            cols = pl.ds(pl.multiple_of(j * TILE, TILE), TILE)
            aproj[:, cols] = jnp.dot(rows[...], aw_v[:, cols], preferred_element_type=F32).astype(BF16)
            return carry

        lax.fori_loop(first, first + (4 if first == 0 else 2), step, 0)

    act_project(a_norm, 0)
    act_project(acot, 4)

    def project(held, low, high, first):
        def step(j, carry):
            cols = pl.ds(pl.multiple_of(j * TILE, TILE), TILE)
            rows = held[low:high].reshape((high - low) * ROWS, D)
            out = jnp.dot(rows, w_v[:, cols], preferred_element_type=F32).astype(BF16)
            proj[low:high, :, cols] = out.reshape(high - low, ROWS, TILE)
            return carry

        lax.fori_loop(first, first + (4 if first == 0 else 2), step, 0)

    right_of[0].wait_send()
    right_of[1].start()
    left_of[1].wait_send()
    left_of[0].start()
    hops[0][2].wait_recv()
    hops[0][4].start()
    hops[1][3].wait_recv()
    hops[1][4].start()
    spread(0, 2)
    spread(1, 3)
    for copy in weights[4:]:
        copy.wait()
    for a in range(2):
        hops[a][1].wait_recv()
        spread(a, 1)
    hops[0][4].wait_send()
    hops[0][5].start()
    hops[1][4].wait_send()
    hops[0][6].start()
    for a in range(2):
        hops[a][4].wait_recv()
        hops[a][7].start()
        spread(a, 4)
    right_of[1].wait_send()
    left_of[0].wait_send()
    hops[1][2].wait_recv()
    hops[0][3].wait_recv()
    spread(1, 2)
    spread(0, 3)
    project(norm_v, 0, 4, 0)
    hops[0][5].wait_send()
    hops[1][5].start()
    hops[0][6].wait_send()
    hops[1][6].start()
    project(cot_v, 0, 4, 4)
    for a, first in ((0, 0), (1, 4)):
        for s in (5, 6, 7):
            hops[a][s].wait_recv()
            spread(a, s)
        project(arrays[a][0], 4, 8, first)

    core = lax.rem(lax.axis_index("dp"), 2)
    seg_v[...] = jnp.broadcast_to(seg[...].astype(F32), (HD, PREF)).T
    seg_rows = jnp.concatenate(
        [seg_v[pl.ds(pl.multiple_of(ROWS * s, ROWS), ROWS), :] for s in slot_order()], 0)
    seg_col, seg_row = seg_rows[:, 0:1], seg_rows.T[0:1, :]
    attend(1 - core, proj, aproj, seg_row, seg_col, grads, agrads, dk, dv)
    theirs = pl.ds(pl.multiple_of((1 - core) * HALF, HALF), HALF)
    act_twins += [
        remote(grads.at[:, theirs], s_grads, act_send.at[2], act_recv.at[2], twin),
        remote(agrads.at[:, theirs], sa_grads, act_send.at[3], act_recv.at[3], twin),
    ]
    for copy in act_twins[2:]:
        copy.start()
    attend(core, proj, aproj, seg_row, seg_col, grads, agrads, dk, dv)
    for a in range(2):
        hops[a][1].wait_send()
        hops[a][7].wait_send()
        for s in range(SLOTS):
            twins[a][s].wait()
            stores[a][s].wait()
    for s in (5, 6):
        hops[1][s].wait_send()
    for copy in act_twins:
        copy.wait()


def gather_and_attend(pin, cot, gain, ain, acot, again, seg, *weights):
    rows = jax.ShapeDtypeStruct((SLOTS, ROWS, D), BF16)
    acts = jax.ShapeDtypeStruct((ACT, DA), BF16)
    dma = pltpu.SemaphoreType.DMA
    return pl.pallas_call(
        gather_kernel,
        out_shape=(
            jax.ShapeDtypeStruct((PREF, COLS), BF16), jax.ShapeDtypeStruct((ACT, COLS), BF16),
            jax.ShapeDtypeStruct((PREF, HALF), BF16), jax.ShapeDtypeStruct((ACT, HALF), BF16),
            rows, rows, rows, rows, acts, acts, acts,
        ),
        in_specs=[VMEM] * 7 + [ANY] * 8,
        out_specs=(VMEM, VMEM, ANY, ANY, ANY, ANY, ANY, ANY, VMEM, ANY, ANY),
        scratch_shapes=[
            pltpu.VMEM((SLOTS, ROWS, D), BF16), pltpu.VMEM((SLOTS, ROWS, D), BF16),
            pltpu.VMEM((D, COLS), BF16), pltpu.VMEM((DA, COLS), BF16),
            pltpu.VMEM((SLOTS, ROWS, COLS), BF16), pltpu.VMEM((ACT, COLS), BF16),
            pltpu.VMEM((PREF, HD), F32), pltpu.VMEM((PREF, HD), F32), pltpu.VMEM((PREF, HD), F32),
            dma((2, SLOTS)), dma((2, SLOTS)), dma((2, SLOTS)), dma((2, SLOTS)), dma((2, SLOTS)),
            dma((8,)), dma((4,)), dma((4,)),
        ],
        compiler_params=pltpu.CompilerParams(
            collective_id=0, has_side_effects=True, vmem_limit_bytes=60 << 20
        ),
        name="gather_and_attend",
    )(pin, cot, gain, ain, acot, again, seg, *weights)


SHARE = 416
PRE, ACTS = 288, 128
Z_PRE, Z_ACT = 4 * PRE, 4 * ACTS
LHS_TILE = 384
UP_TILE = 384
ACT_TILE = 512
HALF_D = D // 2


class Link:
    def __init__(self, window):
        self.window, self.flying = window, []

    def start(self, copy):
        if len(self.flying) == self.window:
            self.flying.pop(0).wait_send()
        copy.start()
        self.flying.append(copy)

    def drain(self):
        for copy in self.flying:
            copy.wait_send()


def add(*terms):
    total = terms[0].astype(F32)
    for term in terms[1:]:
        total = total + term.astype(F32)
    return total


def norm_back(rows, gain, upstream):
    widened = rows.astype(F32)
    inverse = lax.rsqrt(jnp.mean(widened * widened, -1, keepdims=True) + EPSILON)
    normed = widened * inverse
    scaled = upstream * gain
    return (inverse * (scaled - normed * jnp.mean(scaled * normed, -1, keepdims=True))).astype(BF16)


def sum_kernel(
    g_norm, g_cot, s_norm, s_cot, s_grads, a_norm, acot, sa_norm, sa_cot, grads, agrads, sa_grads, pin, gain, ain, again,
    wq, wk, wv, aq, ak, av,
    pgrad, agrad, final,
    left_v, act_v, right_v, aright_v, w_v, part, z1_v, z2_v, h1_v, h2_v, y0_v, y_v, done_v, up_v, u1_v, u2_v, uy_v, aup_v, ay_v, ax_v, gu_v, au_v,
    load_sem, w_sem, ex_sem, z1_send, z1_recv, z2_send, z2_recv, h1_send, h1_recv, h2_send, h2_recv, y0_send, y0_recv, y_send, y_recv, f_send, f_recv, f_local,
    u1_send, u1_recv, u2_send, u2_recv, uy_send, uy_recv, ay_send, ay_recv, ax_send, ax_recv,
):
    d = lax.axis_index("dp")
    z, yh, core = lax.div(d, 4), lax.rem(lax.div(d, 2), 2), lax.rem(d, 2)
    steps = (2, 1, -1, 0)
    z_of = [lax.rem(z + s + 4, 4) for s in steps]

    loads = {}
    for r in range(4):
        for a, pair in enumerate(((g_norm, s_norm), (g_cot, s_cot))):
            cols = pl.ds(pl.multiple_of(z_of[r] * Z_PRE, 128), Z_PRE)
            loads[a, r] = [
                pltpu.make_async_copy(
                    ref.at[:, cols], left_v.at[a, r, pl.ds(PREF * i, PREF)], load_sem.at[a, r, i])
                for i, ref in enumerate(pair)
            ]
    def w_copies(refs, tile, t):
        slot = lax.rem(t, 3)
        rows = pl.ds(pl.multiple_of(t * tile, tile), tile)
        copies = []
        for j, (ref, first) in enumerate(zip(refs, (0, QW, QW + KW))):
            copies.append(pltpu.make_async_copy(
                ref.at[rows], w_v.at[slot, pl.ds(0, tile), pl.ds(first, ref.shape[1])], w_sem.at[slot, j]))
        return copies

    def prime(refs, tile):
        for t in range(2):
            for copy in w_copies(refs, tile, t):
                copy.start()

    z_right, z_left, across, twin = z_step(1), z_step(-1), y_high(), sibling()
    x_right, x_left, x_far, y_near = x_step(1), x_step(-1), x_step(2), y_low()
    mine = pl.ds(pl.multiple_of(core * HALF, HALF), HALF)
    twin_half = pltpu.make_async_copy(s_grads, right_v.at[pl.ds(PREF, PREF)], ex_sem.at[0])
    twin_half.start()
    for copy in loads[0, 0]:
        copy.start()
    prime((aq, ak, av), ACT_TILE)
    for r in range(1, 4):
        for copy in loads[0, r]:
            copy.start()
    right_v[0:PREF] = grads[:, mine]
    aright_v[0:ACT] = agrads[:, mine]
    aright_v[ACT : 2 * ACT] = sa_grads[...]
    act_v[0, 0:ACT] = a_norm[...]
    act_v[0, ACT : 2 * ACT] = sa_norm[...]
    act_v[1, 0:ACT] = acot[...]
    act_v[1, ACT : 2 * ACT] = sa_cot[...]
    twin_half.wait()

    loaded = set()

    def weight_grad(g, r):
        a = 0 if g < 2 else 1
        if (a, r) not in loaded:
            loaded.add((a, r))
            for copy in loads[a, r]:
                copy.wait()
        cols = slice(256 * g, 256 * (g + 1))
        for t in range(Z_PRE // LHS_TILE):
            low, high = t * LHS_TILE, (t + 1) * LHS_TILE
            out = lax.dot_general(
                left_v[a, r, :, low:high], right_v[:, cols], (((0,), (0,)), ((), ())), preferred_element_type=F32
            ).astype(BF16)
            for share in range(4):
                first, last = max(low, PRE * share), min(high, PRE * (share + 1))
                if first < last:
                    part[g, r, share // 2, share % 2, first - PRE * share : last - PRE * share] = (
                        out[first - low : last - low])
        out = lax.dot_general(
            act_v[a, :, pl.ds(pl.multiple_of(z_of[r] * Z_ACT, Z_ACT), Z_ACT)], aright_v[:, cols],
            (((0,), (0,)), ((), ())), preferred_element_type=F32,
        ).astype(BF16)
        for share in range(4):
            part[g, r, share // 2, share % 2, PRE:SHARE] = out[ACTS * share : ACTS * (share + 1)]

    sides = (z_right, z_left)
    z1 = {g: [
        remote(part.at[g, 0, i], z1_v.at[g - 1, i], z1_send.at[g - 1, i], z1_recv.at[g - 1, i], sides[i])
        for i in range(2)] for g in (1, 2)}
    z2 = {g: [[
        remote(part.at[g, 1 + i, y], z2_v.at[g - 1, i, y], z2_send.at[g - 1, i, y], z2_recv.at[g - 1, i, y], sides[i])
        for y in range(2)] for i in range(2)] for g in (1, 2)}
    ys = {g: remote(part.at[g, 3, 1 - yh], y_v.at[g - 1], y_send.at[g - 1], y_recv.at[g - 1], across) for g in (1, 2)}
    y0 = [remote(part.at[0, r, 1 - yh], y0_v.at[r], y0_send.at[r], y0_recv.at[r], across) for r in range(4)]
    h1 = [remote(part.at[0, 0, yh, i], h1_v.at[i], h1_send.at[i], h1_recv.at[i], sides[i]) for i in range(2)]
    h2 = [[
        remote(part.at[0, 1 + i, yh, c], h2_v.at[i, c], h2_send.at[i, c], h2_recv.at[i, c], sides[i])
        for c in range(2)] for i in range(2)]
    outs = [
        remote(done_v.at[g, 1 - core], final.at[core, g], f_send.at[g], f_recv.at[g], twin) for g in range(3)
    ]
    kept = [pltpu.make_async_copy(done_v.at[g, core], final.at[core, g], f_local.at[g]) for g in range(3)]
    z_links, y_link = (Link(2), Link(2)), Link(2)

    def z_first(g, compute=True):
        if compute:
            weight_grad(g, 0)
        for i in range(2):
            z_links[i].start(z1[g][i])

    def z_raw(g):
        for i in range(2):
            weight_grad(g, 1 + i)
            z_links[i].start(z2[g][i][1 - i])

    def z_second(g):
        for i in range(2):
            z1[g][i].wait_recv()
            part[g, 1 + i, i] = add(part[g, 1 + i, i], z1_v[g - 1, i]).astype(BF16)
            z_links[i].start(z2[g][i][i])

    def y_last(g):
        for i in range(2):
            for y in range(2):
                z2[g][i][y].wait_recv()
        y = 1 - yh
        part[g, 3, y] = add(part[g, 3, y], z2_v[g - 1, 0, y], z2_v[g - 1, 1, y]).astype(BF16)
        y_link.start(ys[g])

    def hand_over(g):
        outs[g].start()
        kept[g].start()

    def finish(g):
        ys[g].wait_recv()
        done_v[g] = add(part[g, 3, yh], z2_v[g - 1, 0, yh], z2_v[g - 1, 1, yh], y_v[g - 1]).astype(BF16)
        hand_over(g)

    def y_first(r):
        weight_grad(0, r)
        y_link.start(y0[r])

    def y_add(r):
        y0[r].wait_recv()
        part[0, r, yh] = add(part[0, r, yh], y0_v[r]).astype(BF16)

    def h_first():
        y_add(0)
        for i in range(2):
            z_links[i].start(h1[i])

    def h_raw():
        for i in range(2):
            y_add(1 + i)
            z_links[i].start(h2[i][1 - i])

    def h_second():
        for i in range(2):
            h1[i].wait_recv()
            part[0, 1 + i, yh, i] = add(part[0, 1 + i, yh, i], h1_v[i]).astype(BF16)
            z_links[i].start(h2[i][i])

    def h_finish():
        for i in range(2):
            for c in range(2):
                h2[i][c].wait_recv()
        done_v[0] = add(part[0, 3, yh], h2_v[0], h2_v[1]).astype(BF16)
        hand_over(0)

    def up_loop(refs, tile, first, last, count, use):
        def step(t, carry):
            @pl.when(t + 2 < count)
            def _():
                for copy in w_copies(refs, tile, t + 2):
                    copy.start()

            for copy in w_copies(refs, tile, t):
                copy.wait()
            use(t, lax.rem(t, 3))
            return carry

        lax.fori_loop(first, last, step, 0)

    for h in range(2):
        for first, width, to in ((0, 256, 256 * h), (256, 128, QW + 128 * h), (384, 128, QW + KW + 128 * h)):
            cols = slice(HALF * h + first, HALF * h + first + width)
            gu_v[:, to : to + width] = grads[:, cols]
            au_v[:, to : to + width] = agrads[:, cols]

    def use_pre(t, slot):
        cols = pl.ds(pl.multiple_of(t * UP_TILE, UP_TILE), UP_TILE)
        up_v[:, :, cols] = dot_last(gu_v[...], w_v[slot, 0:UP_TILE]).astype(BF16).reshape(SLOTS, ROWS, UP_TILE)

    def use_act(t, slot):
        cols = pl.ds(pl.multiple_of(t * ACT_TILE, ACT_TILE), ACT_TILE)
        aup_v[:, cols] = dot_last(au_v[...], w_v[slot, 0:ACT_TILE]).astype(BF16)

    def act_loop():
        up_loop((aq, ak, av), ACT_TILE, 0, DA // ACT_TILE, DA // ACT_TILE, use_act)

    def pre_loop(half):
        count = D // UP_TILE
        up_loop((wq, wk, wv), UP_TILE, half * count // 2, (half + 1) * count // 2, count, use_pre)

    u1, u2, uy = [], [], []
    for p in range(2):
        cols = pl.ds(HALF_D * p, HALF_D)
        u1.append([
            remote(up_v.at[s, :, cols], u1_v.at[i, :, cols], u1_send.at[p, i], u1_recv.at[p, i], device)
            for i, (s, device) in enumerate(((4, x_right), (7, x_left)))])
        u2.append([
            remote(up_v.at[s, :, cols], u2_v.at[i, :, cols], u2_send.at[p, i], u2_recv.at[p, i], device)
            for i, (s, device) in enumerate(((3, x_right), (6, x_right), (2, x_left), (5, x_left)))])
        uy.append(remote(up_v.at[1, :, cols], uy_v.at[:, cols], uy_send.at[p], uy_recv.at[p], y_near))
    ay = remote(aup_v, ay_v, ay_send.at[0], ay_recv.at[0], y_near)
    ax = [
        remote(ax_v.at[0], ax_v.at[1 + i], ax_send.at[i], ax_recv.at[i], device)
        for i, device in enumerate((x_right, x_left, x_far))
    ]

    def up_step():
        ay.wait_recv()
        ax_v[0] = add(aup_v[...], ay_v[...]).astype(BF16)
        for copy in ax:
            copy.start()

    def up_start(p):
        pre_loop(p)
        for copy in (u1[p][0], u1[p][1], u2[p][1], u2[p][2]):
            copy.start()

    def up_add(p):
        cols = slice(HALF_D * p, HALF_D * (p + 1))
        for i, s in ((0, 3), (1, 5)):
            u1[p][i].wait_recv()
            up_v[s, :, cols] = add(up_v[s, :, cols], u1_v[i, :, cols]).astype(BF16)
        u2[p][0].start()
        u2[p][3].start()

    def up_last(p):
        cols = slice(HALF_D * p, HALF_D * (p + 1))
        for copy in u2[p]:
            copy.wait_recv()
        up_v[1, :, cols] = add(up_v[1, :, cols], u2_v[1, :, cols], u2_v[3, :, cols]).astype(BF16)
        uy[p].start()

    greet((z_right, z_left, across, twin, x_right, x_left, x_far, y_near), lambda: weight_grad(1, 0))
    z_first(1, compute=False)
    y_first(0)
    act_loop()
    ay.start()
    prime((wq, wk, wv), UP_TILE)
    up_start(0)
    z_raw(1)
    y_first(1)
    up_start(1)
    for key in ((1, 0), (1, 1), (1, 2), (1, 3)):
        for copy in loads[key]:
            copy.start()
    z_first(2)
    y_first(2)
    z_second(1)
    up_add(0)
    y_first(3)
    up_add(1)
    z_raw(2)
    weight_grad(1, 3)
    up_last(0)
    y_last(1)
    weight_grad(2, 3)
    up_last(1)
    up_step()
    z_second(2)
    h_first()
    finish(1)
    y_add(3)
    for copy in uy:
        copy.wait_recv()
    pgrad[...] = norm_back(pin[...], gain[...].reshape(1, D), add(up_v[0], u2_v[0], u2_v[2], uy_v[...]))
    h_raw()
    y_last(2)
    h_second()
    for copy in ax:
        copy.wait_recv()
    agrad[...] = norm_back(ain[...], again[...].reshape(1, DA), add(ax_v[0], ax_v[3]) + add(ax_v[1], ax_v[2]))
    finish(2)
    h_finish()

    for copy in (*u1[0], *u1[1], *u2[0], *u2[1], *uy, ay, *ax):
        copy.wait_send()
    for link in (*z_links, y_link):
        link.drain()
    for g in range(3):
        outs[g].wait()
        kept[g].wait()


def sum_everything(g_norm, g_cot, s_norm, s_cot, *rest):
    wide = tuple(m.reshape(PREF, D) for m in (g_norm, g_cot, s_norm, s_cot))
    dma = pltpu.SemaphoreType.DMA
    share = (2, SHARE, 256)
    row = (ROWS, D)

    def held(*shape):
        return pltpu.VMEM(shape, BF16)

    return pl.pallas_call(
        sum_kernel,
        out_shape=(
            jax.ShapeDtypeStruct(row, BF16), jax.ShapeDtypeStruct((ACT, DA), BF16),
            jax.ShapeDtypeStruct((2, 3, SHARE, 256), BF16),
        ),
        in_specs=[ANY] * 5 + [VMEM] * 11 + [ANY] * 6,
        out_specs=(VMEM, VMEM, ANY),
        scratch_shapes=[
            held(2, 4, 2 * PREF, Z_PRE), held(2, 2 * ACT, DA), held(2 * PREF, HALF), held(2 * ACT, HALF),
            held(3, ACT_TILE, 1024), held(3, 4, 2, *share), held(2, 2, *share), held(2, 2, 2, *share),
            held(*share), held(2, *share), held(4, *share), held(2, *share), held(3, *share), held(SLOTS, *row), held(2, *row), held(4, *row), held(*row),
            held(ACT, DA), held(ACT, DA), held(4, ACT, DA), held(PREF, 1024), held(ACT, 1024),
            dma((2, 4, 2)), dma((3, 3)), dma((1,)), dma((2, 2)), dma((2, 2)), dma((2, 2, 2)), dma((2, 2, 2)),
            dma((2,)), dma((2,)), dma((2, 2)), dma((2, 2)), dma((4,)), dma((4,)),
            dma((2,)), dma((2,)), dma((3,)), dma((3,)), dma((3,)),
            dma((2, 2)), dma((2, 2)), dma((2, 4)), dma((2, 4)), dma((2,)), dma((2,)),
            dma((1,)), dma((1,)), dma((3,)), dma((3,)),
        ],
        compiler_params=pltpu.CompilerParams(
            collective_id=1, has_side_effects=True, vmem_limit_bytes=62 << 20
        ),
        name="sum_everything",
    )(*wide, *rest)


def assemble_kernel(final, pgrad, agrad, *outs):
    outs[0][...] = pgrad[...]
    outs[1][...] = agrad[...]
    at = 2
    for rows in (slice(0, PRE), slice(PRE, SHARE)):
        for g, first, width in ((0, 0, 256), (1, 0, 128), (1, 128, 128), (2, 0, 256)):
            for h in range(2):
                outs[at][:, width * h : width * (h + 1)] = final[h, g, rows, first : first + width]
            at += 1


def assemble(final, pgrad, agrad):
    widths = (QW, KW, KW, QW)
    return pl.pallas_call(
        assemble_kernel,
        out_shape=tuple(
            [jax.ShapeDtypeStruct(pgrad.shape, BF16), jax.ShapeDtypeStruct(agrad.shape, BF16)]
            + [jax.ShapeDtypeStruct((rows, w), BF16) for rows in (PRE, ACTS) for w in widths]),
        in_specs=[VMEM] * 3,
        out_specs=(VMEM,) * 10,
        compiler_params=pltpu.CompilerParams(vmem_limit_bytes=60 << 20),
        name="assemble",
    )(final, pgrad, agrad)


def per_device(prefix_in, action_in, segment_ids, gain_prefix, gain_action, query_prefix, key_prefix, value_prefix,
               out_prefix, query_action, key_action, value_action, out_action, cot_prefix, cot_action):
    grads, agrads, s_grads, sa_grads, g_norm, g_cot, s_norm, s_cot, a_norm, sa_norm, sa_cot = gather_and_attend(
        prefix_in, cot_prefix, gain_prefix, action_in, cot_action, gain_action, segment_ids,
        query_prefix, key_prefix, value_prefix, out_prefix, query_action, key_action, value_action, out_action)
    prefix_grad, action_grad, final = sum_everything(
        g_norm, g_cot, s_norm, s_cot, s_grads, a_norm, cot_action, sa_norm, sa_cot, grads, agrads, sa_grads,
        prefix_in, gain_prefix, action_in, gain_action,
        query_prefix, key_prefix, value_prefix, query_action, key_action, value_action)
    return assemble(final, prefix_grad, action_grad)


def solution(mesh):
    rows, sample, cols = P(("dp", "tensor"), None), P("dp", None), P(None, "tensor")
    in_specs = (rows, sample, sample, P(), P()) + (cols,) * 8 + (rows, sample)
    out_specs = (rows, sample) + (P("dp", "tensor"),) * 8
    return jax.shard_map(per_device, mesh=mesh, in_specs=in_specs, out_specs=out_specs, check_vma=False)
```

```python
import functools
import math

import jax
import jax.numpy as jnp
from jax import lax
from jax.experimental import pallas as pl
from jax.experimental.pallas import tpu as pltpu
from jax.sharding import PartitionSpec as P

D = 4608
DA = 2048
H = 32
HD = 128
ROWS = 64
ACT = 48
SLOTS = 8
PREF = SLOTS * ROWS
QW, KW = 512, 256
COLS = 2 * QW + 2 * KW
HALF = COLS // 2
TILE = 256
EPSILON = 1e-06
SOFT_CAP = 50.0
SCALE = 1.0 / math.sqrt(D // H)
MESH = pl.DeviceIdType.MESH
BF16, F32 = jnp.bfloat16, jnp.float32
VMEM = pl.BlockSpec(memory_space=pltpu.VMEM)
ANY = pl.BlockSpec(memory_space=pl.ANY)


def x_step(k):
    return lax.axis_index("dp"), lax.rem(lax.axis_index("tensor") + 2 * k + 8, 8)


def z_step(k):
    return lax.rem(lax.axis_index("dp") + 4 * k + 16, 16), lax.axis_index("tensor")


def y_low():
    t = lax.axis_index("tensor")
    return lax.axis_index("dp"), t + 1 - 2 * lax.rem(t, 2)


def y_high():
    d = lax.axis_index("dp")
    return d + 2 - 4 * lax.rem(lax.div(d, 2), 2), lax.axis_index("tensor")


def sibling():
    d = lax.axis_index("dp")
    return d + 1 - 2 * lax.rem(d, 2), lax.axis_index("tensor")


def slot_order():
    t = lax.axis_index("tensor")
    x, y = lax.div(t, 2), lax.rem(t, 2)

    def at(step, row):
        return 2 * lax.rem(x + step + 4, 4) + row

    return [at(0, y), at(0, 1 - y), at(-1, y), at(1, y), at(2, y), at(-1, 1 - y), at(1, 1 - y), at(2, 1 - y)]


def greet(partners, meanwhile):
    barrier = pltpu.get_barrier_semaphore()
    for device in partners:
        pl.semaphore_signal(barrier, inc=1, device_id=device, device_id_type=MESH)
    meanwhile()
    pl.semaphore_wait(barrier, len(partners))


def remote(src, dst, send, recv, device):
    return pltpu.make_async_remote_copy(
        src_ref=src, dst_ref=dst, send_sem=send, recv_sem=recv, device_id=device, device_id_type=MESH
    )


def norm(rows, gain):
    widened = rows.astype(F32)
    inverse = lax.rsqrt(jnp.mean(widened * widened, -1, keepdims=True) + EPSILON)
    return (widened * inverse * gain).astype(BF16)


def dot_last(a, b):
    return lax.dot_general(a, b, (((1,), (1,)), ((), ())), preferred_element_type=F32)


def soft(key_rows, query_rows):
    t = jnp.tanh(dot_last(key_rows, query_rows) * (SCALE / SOFT_CAP))
    return t, jnp.exp(SOFT_CAP * t)


BLOCK = 256


def cols(first, width=HD):
    return pl.ds(pl.multiple_of(first, HD), width)


def attend_forward(i, h, proj, seg_row, seg_col, grads, probs, tanhs):
    key = proj[:, :, cols(QW + HD * h)].reshape(PREF, HD)
    value_t = proj[:, :, cols(QW + KW + HD * h)].reshape(PREF, HD).T
    for g in range(2):
        for b in range(PREF // BLOCK):
            rows = slice(b * BLOCK, (b + 1) * BLOCK)
            slots = slice(b * BLOCK // ROWS, (b + 1) * BLOCK // ROWS)
            t, w = soft(key, proj[slots, :, cols(HD * (2 * h + g))].reshape(BLOCK, HD))
            w = jnp.where(seg_col <= seg_row[:, rows], w, 0.0)
            p = w * (1.0 / jnp.sum(w, 0, keepdims=True))
            tanhs[i, g, :, rows] = t
            probs[i, g, :, rows] = p
            at = jnp.dot(value_t, p.astype(BF16), preferred_element_type=F32).T
            grads[rows, cols(HALF * h + 512 + HD * g)] = at.astype(BF16)


def attend(i, h, proj, aproj, probs, tanhs, grads, agrads, dk, dv):
    key = proj[:, :, cols(QW + HD * h)].reshape(PREF, HD)
    value = proj[:, :, cols(QW + KW + HD * h)].reshape(PREF, HD)
    key_t, value_t = key.T, value.T
    base = HALF * h
    akey = aproj[:, cols(QW + HD * h)]
    avalue = aproj[:, cols(QW + KW + HD * h)]

    def two(first):
        return jnp.concatenate([aproj[:, cols(first + HD * (2 * h + g))] for g in range(2)], 0)

    aq, ado = two(0), two(QW + 2 * KW)
    tp, wp = soft(key, aq)
    ta, wa = soft(akey, aq)
    rate = 1.0 / (jnp.sum(wp, 0, keepdims=True) + jnp.sum(wa, 0, keepdims=True))
    pp, pa = wp * rate, wa * rate
    gp, ga = dot_last(value, ado), dot_last(avalue, ado)
    inner = jnp.sum(pp * gp, 0, keepdims=True) + jnp.sum(pa * ga, 0, keepdims=True)
    sp = (pp * (gp - inner) * (1.0 - tp * tp) * SCALE).astype(BF16)
    sa = (pa * (ga - inner) * (1.0 - ta * ta) * SCALE).astype(BF16)
    pp, pa = pp.astype(BF16), pa.astype(BF16)
    dk[...] = jnp.dot(sp, aq, preferred_element_type=F32)
    dv[...] = jnp.dot(pp, ado, preferred_element_type=F32)
    agrads[:, cols(base + 256)] = jnp.dot(sa, aq, preferred_element_type=F32).astype(BF16)
    agrads[:, cols(base + 384)] = jnp.dot(pa, ado, preferred_element_type=F32).astype(BF16)
    adq = (jnp.dot(key_t, sp, preferred_element_type=F32) + jnp.dot(akey.T, sa, preferred_element_type=F32)).T
    aat = (jnp.dot(value_t, pp, preferred_element_type=F32) + jnp.dot(avalue.T, pa, preferred_element_type=F32)).T
    for g in range(2):
        agrads[:, cols(base + HD * g)] = adq[ACT * g : ACT * (g + 1)].astype(BF16)
        agrads[:, cols(base + 512 + HD * g)] = aat[ACT * g : ACT * (g + 1)].astype(BF16)

    for g in range(2):
        for b in range(PREF // BLOCK):
            rows = slice(b * BLOCK, (b + 1) * BLOCK)
            slots = slice(b * BLOCK // ROWS, (b + 1) * BLOCK // ROWS)
            first = HD * (2 * h + g)
            query = proj[slots, :, cols(first)].reshape(BLOCK, HD)
            dout = proj[slots, :, cols(QW + 2 * KW + first)].reshape(BLOCK, HD)
            t, p = tanhs[i, g, :, rows], probs[i, g, :, rows]
            gp = dot_last(value, dout)
            inner = jnp.sum(p * gp, 0, keepdims=True)
            s = (p * (gp - inner) * (1.0 - t * t) * SCALE).astype(BF16)
            dk[...] += jnp.dot(s, query, preferred_element_type=F32)
            dv[...] += jnp.dot(p.astype(BF16), dout, preferred_element_type=F32)
            dq = jnp.dot(key_t, s, preferred_element_type=F32).T
            grads[rows, cols(base + HD * g)] = dq.astype(BF16)
    grads[:, cols(base + 256)] = dk[...].astype(BF16)
    grads[:, cols(base + 384)] = dv[...].astype(BF16)


def gather_kernel(
    pin, cot, gain, ain, acot, again, seg, wq, wk, wv, wo, aq, ak, av, ao,
    grads, agrads, s_grads, sa_grads, g_norm, g_cot, s_norm, s_cot, a_norm, sa_norm, sa_cot,
    norm_v, cot_v, w_v, aw_v, proj, aproj, dk, dv, seg_v, probs, tanhs,
    send, recv, sib_send, sib_recv, local, w_sem, act_send, act_recv,
):
    weights = []
    for i, (ref, first) in enumerate(((aq, 0), (ak, QW), (av, QW + KW), (ao, QW + 2 * KW))):
        weights.append(pltpu.make_async_copy(ref, aw_v.at[:, pl.ds(first, ref.shape[1])], w_sem.at[i]))
    for i, (ref, first) in enumerate(((wq, 0), (wk, QW), (wv, QW + KW), (wo, QW + 2 * KW))):
        weights.append(pltpu.make_async_copy(ref, w_v.at[:, pl.ds(first, ref.shape[1])], w_sem.at[4 + i]))
    for copy in weights:
        copy.start()
    left, right, across, twin = x_step(-1), x_step(1), y_low(), sibling()

    def own_rows():
        cot_v[0] = cot[...]
        norm_v[0] = norm(pin[...], gain[...].reshape(1, D))

    greet((left, right, across, twin), own_rows)

    arrays = ((norm_v, g_norm, s_norm), (cot_v, g_cot, s_cot))

    def hop(a, src, dst, device):
        held = arrays[a][0]
        return remote(held.at[src], held.at[dst], send.at[a, dst], recv.at[a, dst], device)

    hops = [
        {1: hop(a, 0, 1, across), 2: hop(a, 0, 2, right), 3: hop(a, 0, 3, left),
         4: hop(a, 2, 4, right) if a == 0 else hop(a, 3, 4, left),
         5: hop(a, 1, 5, right), 6: hop(a, 1, 6, left), 7: hop(a, 4, 7, across)}
        for a in range(2)
    ]
    twins = [
        [remote(held.at[s], far.at[s], sib_send.at[a, s], sib_recv.at[a, s], twin) for s in range(SLOTS)]
        for a, (held, _, far) in enumerate(arrays)
    ]
    stores = [
        [pltpu.make_async_copy(held.at[s], near.at[s], local.at[a, s]) for s in range(SLOTS)]
        for a, (held, near, _) in enumerate(arrays)
    ]

    def spread(a, s):
        twins[a][s].start()
        stores[a][s].start()

    right_of = (hops[0][2], hops[1][2])
    left_of = (hops[0][3], hops[1][3])
    right_of[0].start()
    left_of[1].start()
    for a in range(2):
        hops[a][1].start()
    spread(1, 0)
    spread(0, 0)

    a_norm[...] = norm(ain[...], again[...].reshape(1, DA))
    act_twins = [
        remote(a_norm, sa_norm, act_send.at[0], act_recv.at[0], twin),
        remote(acot, sa_cot, act_send.at[1], act_recv.at[1], twin),
    ]
    for copy in act_twins:
        copy.start()
    for copy in weights[:4]:
        copy.wait()

    def act_project(rows, first):
        def step(j, carry):
            cols = pl.ds(pl.multiple_of(j * TILE, TILE), TILE)
            aproj[:, cols] = jnp.dot(rows[...], aw_v[:, cols], preferred_element_type=F32).astype(BF16)
            return carry

        lax.fori_loop(first, first + (4 if first == 0 else 2), step, 0)

    act_project(a_norm, 0)
    act_project(acot, 4)

    def project(held, low, high, first):
        def step(j, carry):
            cols = pl.ds(pl.multiple_of(j * TILE, TILE), TILE)
            rows = held[low:high].reshape((high - low) * ROWS, D)
            out = jnp.dot(rows, w_v[:, cols], preferred_element_type=F32).astype(BF16)
            proj[low:high, :, cols] = out.reshape(high - low, ROWS, TILE)
            return carry

        lax.fori_loop(first, first + (4 if first == 0 else 2), step, 0)

    right_of[0].wait_send()
    right_of[1].start()
    left_of[1].wait_send()
    left_of[0].start()
    hops[0][2].wait_recv()
    hops[0][4].start()
    hops[1][3].wait_recv()
    hops[1][4].start()
    spread(0, 2)
    spread(1, 3)
    for copy in weights[4:]:
        copy.wait()
    for a in range(2):
        hops[a][1].wait_recv()
        spread(a, 1)
    hops[0][4].wait_send()
    hops[0][5].start()
    hops[1][4].wait_send()
    hops[0][6].start()
    hops[1][5].start()
    hops[1][6].start()
    for a in range(2):
        hops[a][4].wait_recv()
        hops[a][7].start()
        spread(a, 4)
    right_of[1].wait_send()
    left_of[0].wait_send()
    hops[1][2].wait_recv()
    hops[0][3].wait_recv()
    spread(1, 2)
    spread(0, 3)
    project(norm_v, 0, 4, 0)
    project(cot_v, 0, 4, 4)
    for s in (5, 6):
        hops[0][s].wait_send()
    core = lax.rem(lax.axis_index("dp"), 2)
    seg_v[...] = jnp.broadcast_to(seg[...].astype(F32), (HD, PREF)).T
    seg_rows = jnp.concatenate(
        [seg_v[pl.ds(pl.multiple_of(ROWS * s, ROWS), ROWS), :] for s in slot_order()], 0)
    seg_col, seg_row = seg_rows[:, 0:1], seg_rows.T[0:1, :]
    for a, first in ((0, 0), (1, 4)):
        for s in (5, 6, 7):
            hops[a][s].wait_recv()
            spread(a, s)
        project(arrays[a][0], 4, 8, first)
        if a == 0:
            for i, h in enumerate((1 - core, core)):
                attend_forward(i, h, proj, seg_row, seg_col, grads, probs, tanhs)

    attend(0, 1 - core, proj, aproj, probs, tanhs, grads, agrads, dk, dv)
    theirs = pl.ds(pl.multiple_of((1 - core) * HALF, HALF), HALF)
    act_twins += [
        remote(grads.at[:, theirs], s_grads, act_send.at[2], act_recv.at[2], twin),
        remote(agrads.at[:, theirs], sa_grads, act_send.at[3], act_recv.at[3], twin),
    ]
    for copy in act_twins[2:]:
        copy.start()
    attend(1, core, proj, aproj, probs, tanhs, grads, agrads, dk, dv)
    for a in range(2):
        hops[a][1].wait_send()
        hops[a][7].wait_send()
        for s in range(SLOTS):
            twins[a][s].wait()
            stores[a][s].wait()
    for s in (5, 6):
        hops[1][s].wait_send()
    for copy in act_twins:
        copy.wait()


def gather_and_attend(pin, cot, gain, ain, acot, again, seg, *weights):
    rows = jax.ShapeDtypeStruct((SLOTS, ROWS, D), BF16)
    acts = jax.ShapeDtypeStruct((ACT, DA), BF16)
    dma = pltpu.SemaphoreType.DMA
    return pl.pallas_call(
        gather_kernel,
        out_shape=(
            jax.ShapeDtypeStruct((PREF, COLS), BF16), jax.ShapeDtypeStruct((ACT, COLS), BF16),
            jax.ShapeDtypeStruct((PREF, HALF), BF16), jax.ShapeDtypeStruct((ACT, HALF), BF16),
            rows, rows, rows, rows, acts, acts, acts,
        ),
        in_specs=[VMEM] * 7 + [ANY] * 8,
        out_specs=(VMEM, VMEM, ANY, ANY, ANY, ANY, ANY, ANY, VMEM, ANY, ANY),
        scratch_shapes=[
            pltpu.VMEM((SLOTS, ROWS, D), BF16), pltpu.VMEM((SLOTS, ROWS, D), BF16),
            pltpu.VMEM((D, COLS), BF16), pltpu.VMEM((DA, COLS), BF16),
            pltpu.VMEM((SLOTS, ROWS, COLS), BF16), pltpu.VMEM((ACT, COLS), BF16),
            pltpu.VMEM((PREF, HD), F32), pltpu.VMEM((PREF, HD), F32), pltpu.VMEM((PREF, HD), F32),
            pltpu.VMEM((2, 2, PREF, PREF), F32), pltpu.VMEM((2, 2, PREF, PREF), F32),
            dma((2, SLOTS)), dma((2, SLOTS)), dma((2, SLOTS)), dma((2, SLOTS)), dma((2, SLOTS)),
            dma((8,)), dma((4,)), dma((4,)),
        ],
        compiler_params=pltpu.CompilerParams(
            collective_id=0, has_side_effects=True, vmem_limit_bytes=60 << 20
        ),
        name="gather_and_attend",
    )(pin, cot, gain, ain, acot, again, seg, *weights)


SHARE = 416
PRE, ACTS = 288, 128
Z_PRE, Z_ACT = 4 * PRE, 4 * ACTS
LHS_TILE = 384
UP_TILE = 384
ACT_TILE = 512
HALF_D = D // 2


class Link:
    def __init__(self, window):
        self.window, self.flying = window, []

    def start(self, copy):
        if len(self.flying) == self.window:
            self.flying.pop(0).wait_send()
        copy.start()
        self.flying.append(copy)

    def drain(self):
        for copy in self.flying:
            copy.wait_send()


def add(*terms):
    total = terms[0].astype(F32)
    for term in terms[1:]:
        total = total + term.astype(F32)
    return total


def norm_back(rows, gain, upstream):
    widened = rows.astype(F32)
    inverse = lax.rsqrt(jnp.mean(widened * widened, -1, keepdims=True) + EPSILON)
    normed = widened * inverse
    scaled = upstream * gain
    return (inverse * (scaled - normed * jnp.mean(scaled * normed, -1, keepdims=True))).astype(BF16)


def sum_kernel(
    g_norm, g_cot, s_norm, s_cot, s_grads, a_norm, acot, sa_norm, sa_cot, grads, agrads, sa_grads, pin, gain, ain, again,
    wq, wk, wv, aq, ak, av,
    pgrad, agrad, final,
    left_v, act_v, right_v, aright_v, w_v, part, z1_v, z2_v, h1_v, h2_v, y0_v, y_v, done_v, up_v, u1_v, u2_v, uy_v, aup_v, ay_v, ax_v, gu_v, au_v,
    load_sem, w_sem, ex_sem, z1_send, z1_recv, z2_send, z2_recv, h1_send, h1_recv, h2_send, h2_recv, y0_send, y0_recv, y_send, y_recv, f_send, f_recv, f_local,
    u1_send, u1_recv, u2_send, u2_recv, uy_send, uy_recv, ay_send, ay_recv, ax_send, ax_recv,
):
    d = lax.axis_index("dp")
    z, yh, core = lax.div(d, 4), lax.rem(lax.div(d, 2), 2), lax.rem(d, 2)
    steps = (2, 1, -1, 0)
    z_of = [lax.rem(z + s + 4, 4) for s in steps]

    loads = {}
    for r in range(4):
        for a, pair in enumerate(((g_norm, s_norm), (g_cot, s_cot))):
            cols = pl.ds(pl.multiple_of(z_of[r] * Z_PRE, 128), Z_PRE)
            loads[a, r] = [
                pltpu.make_async_copy(
                    ref.at[:, cols], left_v.at[a, r, pl.ds(PREF * i, PREF)], load_sem.at[a, r, i])
                for i, ref in enumerate(pair)
            ]
    def w_copies(refs, tile, t):
        slot = lax.rem(t, 3)
        rows = pl.ds(pl.multiple_of(t * tile, tile), tile)
        copies = []
        for j, (ref, first) in enumerate(zip(refs, (0, QW, QW + KW))):
            copies.append(pltpu.make_async_copy(
                ref.at[rows], w_v.at[slot, pl.ds(0, tile), pl.ds(first, ref.shape[1])], w_sem.at[slot, j]))
        return copies

    def prime(refs, tile):
        for t in range(2):
            for copy in w_copies(refs, tile, t):
                copy.start()

    z_right, z_left, across, twin = z_step(1), z_step(-1), y_high(), sibling()
    x_right, x_left, x_far, y_near = x_step(1), x_step(-1), x_step(2), y_low()
    mine = pl.ds(pl.multiple_of(core * HALF, HALF), HALF)
    twin_half = pltpu.make_async_copy(s_grads, right_v.at[pl.ds(PREF, PREF)], ex_sem.at[0])
    twin_half.start()
    for copy in loads[0, 0]:
        copy.start()
    prime((aq, ak, av), ACT_TILE)
    for r in range(1, 4):
        for copy in loads[0, r]:
            copy.start()
    right_v[0:PREF] = grads[:, mine]
    aright_v[0:ACT] = agrads[:, mine]
    aright_v[ACT : 2 * ACT] = sa_grads[...]
    act_v[0, 0:ACT] = a_norm[...]
    act_v[0, ACT : 2 * ACT] = sa_norm[...]
    act_v[1, 0:ACT] = acot[...]
    act_v[1, ACT : 2 * ACT] = sa_cot[...]
    twin_half.wait()

    loaded = set()

    def weight_grad(g, r):
        a = 0 if g < 2 else 1
        if (a, r) not in loaded:
            loaded.add((a, r))
            for copy in loads[a, r]:
                copy.wait()
        cols = slice(256 * g, 256 * (g + 1))
        for t in range(Z_PRE // LHS_TILE):
            low, high = t * LHS_TILE, (t + 1) * LHS_TILE
            out = lax.dot_general(
                left_v[a, r, :, low:high], right_v[:, cols], (((0,), (0,)), ((), ())), preferred_element_type=F32
            ).astype(BF16)
            for share in range(4):
                first, last = max(low, PRE * share), min(high, PRE * (share + 1))
                if first < last:
                    part[g, r, share // 2, share % 2, first - PRE * share : last - PRE * share] = (
                        out[first - low : last - low])
        out = lax.dot_general(
            act_v[a, :, pl.ds(pl.multiple_of(z_of[r] * Z_ACT, Z_ACT), Z_ACT)], aright_v[:, cols],
            (((0,), (0,)), ((), ())), preferred_element_type=F32,
        ).astype(BF16)
        for share in range(4):
            part[g, r, share // 2, share % 2, PRE:SHARE] = out[ACTS * share : ACTS * (share + 1)]

    sides = (z_right, z_left)
    z1 = {g: [
        remote(part.at[g, 0, i], z1_v.at[g - 1, i], z1_send.at[g - 1, i], z1_recv.at[g - 1, i], sides[i])
        for i in range(2)] for g in (1, 2)}
    z2 = {g: [[
        remote(part.at[g, 1 + i, y], z2_v.at[g - 1, i, y], z2_send.at[g - 1, i, y], z2_recv.at[g - 1, i, y], sides[i])
        for y in range(2)] for i in range(2)] for g in (1, 2)}
    ys = {g: remote(part.at[g, 3, 1 - yh], y_v.at[g - 1], y_send.at[g - 1], y_recv.at[g - 1], across) for g in (1, 2)}
    y0 = [remote(part.at[0, r, 1 - yh], y0_v.at[r], y0_send.at[r], y0_recv.at[r], across) for r in range(4)]
    h1 = [remote(part.at[0, 0, yh, i], h1_v.at[i], h1_send.at[i], h1_recv.at[i], sides[i]) for i in range(2)]
    h2 = [[
        remote(part.at[0, 1 + i, yh, c], h2_v.at[i, c], h2_send.at[i, c], h2_recv.at[i, c], sides[i])
        for c in range(2)] for i in range(2)]
    outs = [
        remote(done_v.at[g, 1 - core], final.at[core, g], f_send.at[g], f_recv.at[g], twin) for g in range(3)
    ]
    kept = [pltpu.make_async_copy(done_v.at[g, core], final.at[core, g], f_local.at[g]) for g in range(3)]
    z_links, y_link = (Link(2), Link(2)), Link(2)

    def z_first(g, compute=True):
        if compute:
            weight_grad(g, 0)
        for i in range(2):
            z_links[i].start(z1[g][i])

    def z_raw(g):
        for i in range(2):
            weight_grad(g, 1 + i)
            z_links[i].start(z2[g][i][1 - i])

    def z_second(g):
        for i in range(2):
            z1[g][i].wait_recv()
            part[g, 1 + i, i] = add(part[g, 1 + i, i], z1_v[g - 1, i]).astype(BF16)
            z_links[i].start(z2[g][i][i])

    def y_last(g):
        for i in range(2):
            for y in range(2):
                z2[g][i][y].wait_recv()
        y = 1 - yh
        part[g, 3, y] = add(part[g, 3, y], z2_v[g - 1, 0, y], z2_v[g - 1, 1, y]).astype(BF16)
        y_link.start(ys[g])

    def hand_over(g):
        outs[g].start()
        kept[g].start()

    def finish(g):
        ys[g].wait_recv()
        done_v[g] = add(part[g, 3, yh], z2_v[g - 1, 0, yh], z2_v[g - 1, 1, yh], y_v[g - 1]).astype(BF16)
        hand_over(g)

    def y_first(r):
        weight_grad(0, r)
        y_link.start(y0[r])

    def y_add(r):
        y0[r].wait_recv()
        part[0, r, yh] = add(part[0, r, yh], y0_v[r]).astype(BF16)

    def h_first():
        y_add(0)
        for i in range(2):
            z_links[i].start(h1[i])

    def h_raw():
        for i in range(2):
            y_add(1 + i)
            z_links[i].start(h2[i][1 - i])

    def h_second():
        for i in range(2):
            h1[i].wait_recv()
            part[0, 1 + i, yh, i] = add(part[0, 1 + i, yh, i], h1_v[i]).astype(BF16)
            z_links[i].start(h2[i][i])

    def h_finish():
        for i in range(2):
            for c in range(2):
                h2[i][c].wait_recv()
        done_v[0] = add(part[0, 3, yh], h2_v[0], h2_v[1]).astype(BF16)
        hand_over(0)

    def up_loop(refs, tile, first, last, count, use):
        def step(t, carry):
            @pl.when(t + 2 < count)
            def _():
                for copy in w_copies(refs, tile, t + 2):
                    copy.start()

            for copy in w_copies(refs, tile, t):
                copy.wait()
            use(t, lax.rem(t, 3))
            return carry

        lax.fori_loop(first, last, step, 0)

    for h in range(2):
        for first, width, to in ((0, 256, 256 * h), (256, 128, QW + 128 * h), (384, 128, QW + KW + 128 * h)):
            cols = slice(HALF * h + first, HALF * h + first + width)
            gu_v[:, to : to + width] = grads[:, cols]
            au_v[:, to : to + width] = agrads[:, cols]

    def use_pre(t, slot):
        cols = pl.ds(pl.multiple_of(t * UP_TILE, UP_TILE), UP_TILE)
        up_v[:, :, cols] = dot_last(gu_v[...], w_v[slot, 0:UP_TILE]).astype(BF16).reshape(SLOTS, ROWS, UP_TILE)

    def use_act(t, slot):
        cols = pl.ds(pl.multiple_of(t * ACT_TILE, ACT_TILE), ACT_TILE)
        aup_v[:, cols] = dot_last(au_v[...], w_v[slot, 0:ACT_TILE]).astype(BF16)

    def act_loop():
        up_loop((aq, ak, av), ACT_TILE, 0, DA // ACT_TILE, DA // ACT_TILE, use_act)

    def pre_loop(half):
        count = D // UP_TILE
        up_loop((wq, wk, wv), UP_TILE, half * count // 2, (half + 1) * count // 2, count, use_pre)

    u1, u2, uy = [], [], []
    for p in range(2):
        cols = pl.ds(HALF_D * p, HALF_D)
        u1.append([
            remote(up_v.at[s, :, cols], u1_v.at[i, :, cols], u1_send.at[p, i], u1_recv.at[p, i], device)
            for i, (s, device) in enumerate(((4, x_right), (7, x_left)))])
        u2.append([
            remote(up_v.at[s, :, cols], u2_v.at[i, :, cols], u2_send.at[p, i], u2_recv.at[p, i], device)
            for i, (s, device) in enumerate(((3, x_right), (6, x_right), (2, x_left), (5, x_left)))])
        uy.append(remote(up_v.at[1, :, cols], uy_v.at[:, cols], uy_send.at[p], uy_recv.at[p], y_near))
    ay = remote(aup_v, ay_v, ay_send.at[0], ay_recv.at[0], y_near)
    ax = [
        remote(ax_v.at[0], ax_v.at[1 + i], ax_send.at[i], ax_recv.at[i], device)
        for i, device in enumerate((x_right, x_left, x_far))
    ]

    def up_step():
        ay.wait_recv()
        ax_v[0] = add(aup_v[...], ay_v[...]).astype(BF16)
        for copy in ax:
            copy.start()

    def up_start(p):
        pre_loop(p)
        for copy in (u1[p][0], u1[p][1], u2[p][1], u2[p][2]):
            copy.start()

    def up_add(p):
        cols = slice(HALF_D * p, HALF_D * (p + 1))
        for i, s in ((0, 3), (1, 5)):
            u1[p][i].wait_recv()
            up_v[s, :, cols] = add(up_v[s, :, cols], u1_v[i, :, cols]).astype(BF16)
        u2[p][0].start()
        u2[p][3].start()

    def up_last(p):
        cols = slice(HALF_D * p, HALF_D * (p + 1))
        for copy in u2[p]:
            copy.wait_recv()
        up_v[1, :, cols] = add(up_v[1, :, cols], u2_v[1, :, cols], u2_v[3, :, cols]).astype(BF16)
        uy[p].start()

    greet((z_right, z_left, across, twin, x_right, x_left, x_far, y_near), lambda: weight_grad(1, 0))
    z_first(1, compute=False)
    y_first(0)
    act_loop()
    ay.start()
    prime((wq, wk, wv), UP_TILE)
    up_start(0)
    z_raw(1)
    y_first(1)
    up_start(1)
    for key in ((1, 0), (1, 1), (1, 2), (1, 3)):
        for copy in loads[key]:
            copy.start()
    z_first(2)
    y_first(2)
    z_second(1)
    up_add(0)
    y_first(3)
    up_add(1)
    z_raw(2)
    weight_grad(1, 3)
    up_last(0)
    y_last(1)
    weight_grad(2, 3)
    up_last(1)
    up_step()
    z_second(2)
    h_first()
    finish(1)
    y_add(3)
    for copy in uy:
        copy.wait_recv()
    pgrad[...] = norm_back(pin[...], gain[...].reshape(1, D), add(up_v[0], u2_v[0], u2_v[2], uy_v[...]))
    h_raw()
    y_last(2)
    h_second()
    for copy in ax:
        copy.wait_recv()
    agrad[...] = norm_back(ain[...], again[...].reshape(1, DA), add(ax_v[0], ax_v[3]) + add(ax_v[1], ax_v[2]))
    finish(2)
    h_finish()

    for copy in (*u1[0], *u1[1], *u2[0], *u2[1], *uy, ay, *ax):
        copy.wait_send()
    for link in (*z_links, y_link):
        link.drain()
    for g in range(3):
        outs[g].wait()
        kept[g].wait()


def sum_everything(g_norm, g_cot, s_norm, s_cot, *rest):
    wide = tuple(m.reshape(PREF, D) for m in (g_norm, g_cot, s_norm, s_cot))
    dma = pltpu.SemaphoreType.DMA
    share = (2, SHARE, 256)
    row = (ROWS, D)

    def held(*shape):
        return pltpu.VMEM(shape, BF16)

    return pl.pallas_call(
        sum_kernel,
        out_shape=(
            jax.ShapeDtypeStruct(row, BF16), jax.ShapeDtypeStruct((ACT, DA), BF16),
            jax.ShapeDtypeStruct((2, 3, SHARE, 256), BF16),
        ),
        in_specs=[ANY] * 5 + [VMEM] * 11 + [ANY] * 6,
        out_specs=(VMEM, VMEM, ANY),
        scratch_shapes=[
            held(2, 4, 2 * PREF, Z_PRE), held(2, 2 * ACT, DA), held(2 * PREF, HALF), held(2 * ACT, HALF),
            held(3, ACT_TILE, 1024), held(3, 4, 2, *share), held(2, 2, *share), held(2, 2, 2, *share),
            held(*share), held(2, *share), held(4, *share), held(2, *share), held(3, *share), held(SLOTS, *row), held(2, *row), held(4, *row), held(*row),
            held(ACT, DA), held(ACT, DA), held(4, ACT, DA), held(PREF, 1024), held(ACT, 1024),
            dma((2, 4, 2)), dma((3, 3)), dma((1,)), dma((2, 2)), dma((2, 2)), dma((2, 2, 2)), dma((2, 2, 2)),
            dma((2,)), dma((2,)), dma((2, 2)), dma((2, 2)), dma((4,)), dma((4,)),
            dma((2,)), dma((2,)), dma((3,)), dma((3,)), dma((3,)),
            dma((2, 2)), dma((2, 2)), dma((2, 4)), dma((2, 4)), dma((2,)), dma((2,)),
            dma((1,)), dma((1,)), dma((3,)), dma((3,)),
        ],
        compiler_params=pltpu.CompilerParams(
            collective_id=1, has_side_effects=True, vmem_limit_bytes=62 << 20
        ),
        name="sum_everything",
    )(*wide, *rest)


def assemble_kernel(final, pgrad, agrad, *outs):
    outs[0][...] = pgrad[...]
    outs[1][...] = agrad[...]
    at = 2
    for rows in (slice(0, PRE), slice(PRE, SHARE)):
        for g, first, width in ((0, 0, 256), (1, 0, 128), (1, 128, 128), (2, 0, 256)):
            for h in range(2):
                outs[at][:, width * h : width * (h + 1)] = final[h, g, rows, first : first + width]
            at += 1


def assemble(final, pgrad, agrad):
    widths = (QW, KW, KW, QW)
    return pl.pallas_call(
        assemble_kernel,
        out_shape=tuple(
            [jax.ShapeDtypeStruct(pgrad.shape, BF16), jax.ShapeDtypeStruct(agrad.shape, BF16)]
            + [jax.ShapeDtypeStruct((rows, w), BF16) for rows in (PRE, ACTS) for w in widths]),
        in_specs=[VMEM] * 3,
        out_specs=(VMEM,) * 10,
        compiler_params=pltpu.CompilerParams(vmem_limit_bytes=60 << 20),
        name="assemble",
    )(final, pgrad, agrad)


def per_device(prefix_in, action_in, segment_ids, gain_prefix, gain_action, query_prefix, key_prefix, value_prefix,
               out_prefix, query_action, key_action, value_action, out_action, cot_prefix, cot_action):
    grads, agrads, s_grads, sa_grads, g_norm, g_cot, s_norm, s_cot, a_norm, sa_norm, sa_cot = gather_and_attend(
        prefix_in, cot_prefix, gain_prefix, action_in, cot_action, gain_action, segment_ids,
        query_prefix, key_prefix, value_prefix, out_prefix, query_action, key_action, value_action, out_action)
    prefix_grad, action_grad, final = sum_everything(
        g_norm, g_cot, s_norm, s_cot, s_grads, a_norm, cot_action, sa_norm, sa_cot, grads, agrads, sa_grads,
        prefix_in, gain_prefix, action_in, gain_action,
        query_prefix, key_prefix, value_prefix, query_action, key_action, value_action)
    return assemble(final, prefix_grad, action_grad)


def solution(mesh):
    rows, sample, cols = P(("dp", "tensor"), None), P("dp", None), P(None, "tensor")
    in_specs = (rows, sample, sample, P(), P()) + (cols,) * 8 + (rows, sample)
    out_specs = (rows, sample) + (P("dp", "tensor"),) * 8
    return jax.shard_map(per_device, mesh=mesh, in_specs=in_specs, out_specs=out_specs, check_vma=False)
```
